512 devices in a mesh: leaf: 128 (over y, z, core), rhs: 4 (over x).
Axes of the slice: x: 4, y: 8, z: 8, core: 2. Of those that a mesh axis runs over, the one named last changes fastest.
Arguments:
- rhs_block: bfloat16 [128, 1048576], P('rhs', 'leaf'), may hold values from -6 to 6
- points: float32 [32, 1048576], P(None, 'leaf'), may hold values from -1.5 to 1.5
- basis: bfloat16 [2048, 512, 128], P('leaf'), may hold values from -0.25 to 0.25
- skeleton_leaf: int32 [2048, 128], P('leaf'), may hold values from 0 to 511, as said below
- skeleton_lower: int32 [512, 128], P('leaf'), may hold values from 0 to 511, as said below
- skeleton_upper: int32 [128, 128], P('leaf'), may hold values from 0 to 511, as said below
- skeleton_top: int32 [32, 128], replicated, may hold values from 0 to 511, as said below
- transfer_leaf: bfloat16 [2048, 128, 128], P('leaf'), may hold values from -0.25 to 0.25
- transfer_lower: bfloat16 [512, 128, 128], P('leaf'), may hold values from -0.25 to 0.25
- transfer_upper: bfloat16 [128, 128, 128], P('leaf'), may hold values from -0.25 to 0.25
Outputs:
- product: bfloat16 [128, 1048576], P('rhs', 'leaf')
The draws below stay inside these ranges and needn't reach their ends.
Inputs may be any that keep to these rules, and one draw needn't show every extreme that they name: `skeleton_leaf`: the 128 entries of a row are distinct rows of the leaf. `skeleton_lower`: the 128 entries of a row are distinct. `skeleton_upper`: the 128 entries of a row are distinct. `skeleton_top`: the 128 entries of a row are distinct.
All inputs are finite; a program needn't handle non-finite values.
Results may differ from the reference program's by a relative error of at most 0.0038.
The reference program's roundings to bfloat16 on the way (of `block` and `near`) count: a program that leaves them out, or rounds other values in their place, can miss the bound.
Values may be sent and summed in bfloat16 or wider, within the bound.
No kernel may reach another device: no remote copies, remote signals or barrier semaphores. Data moves between devices by JAX's collectives and lax.ppermute only.
A program may use at most 64 MiB of HBM per device.

```python
import jax
import jax.numpy as jnp
from jax import lax

COLUMNS = 128
DIMS = 32
LEAF = 512
RANK = 128
LEAVES = 2048
POINTS = 1048576
LOWER = 512
UPPER = 128
TOPS = 32


def skeleton_rows(key, count, total):

    def one_row(row_key):
        first_key, second_key = jax.random.split(row_key)
        rest = jax.random.permutation(first_key, total - 2).astype(jnp.int32) + 1
        ends = jnp.array([0, total - 1], jnp.int32)
        row = jnp.concatenate([ends, rest[:RANK - 2]])
        return row[jax.random.permutation(second_key, RANK)]
    return jax.vmap(one_row)(jax.random.split(key, count))


def draw_skeleton_leaf(key, part):
    key = jax.random.fold_in(key, 11)
    return skeleton_rows(key, LEAVES, LEAF)


def draw_skeleton_lower(key, part):
    key = jax.random.fold_in(key, 12)
    return skeleton_rows(key, LOWER, 4 * RANK)


def draw_skeleton_upper(key, part):
    key = jax.random.fold_in(key, 13)
    return skeleton_rows(key, UPPER, 4 * RANK)


def draw_skeleton_top(key, part):
    key = jax.random.fold_in(key, 14)
    return skeleton_rows(key, TOPS, 4 * RANK)


def shard_levels(rng, shape, cuts, smallest, largest):
    def one(dim, blocks):
        draws = jax.random.uniform(jax.random.fold_in(jax.random.fold_in(rng, 6), dim), (blocks,), jnp.float32, smallest / len(cuts), largest / len(cuts))
        return jnp.repeat(jnp.exp(draws), shape[dim] // blocks).reshape((-1,) + (1,) * (len(shape) - dim - 1))

    factor_of = one(*cuts[0])
    for cut in cuts[1:]:
        factor_of = factor_of * one(*cut)
    return factor_of


def centred(key, shape, width, bound, cuts=(), kind=jnp.bfloat16):
    loudness = shard_levels(key, shape, cuts, -0.22, 0.18) if cuts else 1.0
    entries = jax.random.normal(key, shape, jnp.float32) * width * loudness
    return jnp.minimum(jnp.maximum(entries, -bound), bound).astype(kind)


def setup_inputs(seed: int = 0) -> dict:
    splits = jax.random.split(jax.random.key(seed), 11)
    return {
        "rhs_block": centred(splits[0], (COLUMNS, POINTS), 1.0, 6.0, ((0, 4), (1, 128))),
        "points": centred(splits[1], (DIMS, POINTS), 0.25, 1.5, ((1, 128),), jnp.float32),
        "basis": centred(splits[2], (LEAVES, LEAF, RANK), LEAF ** -0.5, 0.25, ((0, 128),)),
        "skeleton_leaf": draw_skeleton_leaf(jax.random.fold_in(splits[10], 71), 0),
        "skeleton_lower": draw_skeleton_lower(jax.random.fold_in(splits[10], 71), 0),
        "skeleton_upper": draw_skeleton_upper(jax.random.fold_in(splits[10], 71), 0),
        "skeleton_top": draw_skeleton_top(jax.random.fold_in(splits[10], 71), 0),
        "transfer_leaf": centred(splits[7], (LEAVES, RANK, RANK), (4 * RANK) ** -0.5, 0.25, ((0, 128),)),
        "transfer_lower": centred(splits[8], (LOWER, RANK, RANK), (4 * RANK) ** -0.5, 0.25, ((0, 128),)),
        "transfer_upper": centred(splits[9], (UPPER, RANK, RANK), (4 * RANK) ** -0.5, 0.25, ((0, 128),)),
    }


RIDGE = 1.0
HIGH = lax.Precision.HIGHEST


def kernel_block(left, right):
    left_sq = jnp.sum(left * left, axis=0)
    right_sq = jnp.sum(right * right, axis=0)
    cross = jnp.dot(left.T, right, precision=HIGH, preferred_element_type=jnp.float32)
    return jnp.exp(-(left_sq[:, None] + right_sq[None, :] - 2.0 * cross))


def sibling_terms(coeffs, places):
    count = coeffs.shape[0] // 4
    grouped = (coeffs.reshape((count, 4) + coeffs.shape[1:]), places.reshape((count, 4) + places.shape[1:]))

    def per_group(pair):
        group_coeffs, group_places = pair
        result = []
        for target in range(4):
            total = jnp.zeros(group_coeffs.shape[1:], jnp.float32)
            for source in range(4):
                if source != target:
                    total = total + jnp.dot(group_coeffs[source], kernel_block(group_places[source], group_places[target]), precision=HIGH, preferred_element_type=jnp.float32)
            result.append(total)
        return jnp.stack(result)

    return lax.map(per_group, grouped).reshape(coeffs.shape)


def parent_places(places, index):
    count = places.shape[0] // 4
    dims_here, rank_here = places.shape[1], places.shape[2]
    candidates = places.reshape(count, 4, dims_here, rank_here).transpose(0, 2, 1, 3).reshape(count, dims_here, 4 * rank_here)
    return jnp.take_along_axis(candidates, index[:, None, :], axis=2)


def lift(coeffs, transfer):
    moved = jnp.einsum('nrk,nkm->nrm', coeffs, transfer.astype(jnp.float32), precision=HIGH)
    count = coeffs.shape[0] // 4
    return moved.reshape((count, 4) + moved.shape[1:]).sum(axis=1)


def descend(parent_terms, transfer, local_terms):
    repeated = jnp.repeat(parent_terms, 4, axis=0)
    return local_terms + jnp.einsum('nrm,nkm->nrk', repeated, transfer.astype(jnp.float32), precision=HIGH)


def reference(rhs_block, points, basis, skeleton_leaf, skeleton_lower, skeleton_upper, skeleton_top, transfer_leaf, transfer_lower, transfer_upper):
    leaf_points = points.reshape(DIMS, LEAVES, LEAF).transpose(1, 0, 2)
    leaf_rhs = rhs_block.reshape(COLUMNS, LEAVES, LEAF).transpose(1, 0, 2)

    def leaf_near(pair):
        place, values = pair
        block = kernel_block(place, place).astype(jnp.bfloat16)
        total = jnp.dot(values, block, preferred_element_type=jnp.float32) + RIDGE * values.astype(jnp.float32)
        return total.astype(jnp.bfloat16)

    near = lax.map(leaf_near, (leaf_points, leaf_rhs))
    coeff_leaf = lax.map(lambda pair: jnp.dot(pair[0], pair[1], preferred_element_type=jnp.float32), (leaf_rhs, basis))
    place_leaf = jnp.take_along_axis(leaf_points, skeleton_leaf[:, None, :], axis=2)
    coeff_lower = lift(coeff_leaf, transfer_leaf)
    place_lower = parent_places(place_leaf, skeleton_lower)
    coeff_upper = lift(coeff_lower, transfer_lower)
    place_upper = parent_places(place_lower, skeleton_upper)
    coeff_top = lift(coeff_upper, transfer_upper)
    place_top = parent_places(place_upper, skeleton_top)
    leaf_terms = sibling_terms(coeff_leaf, place_leaf)
    lower_terms = sibling_terms(coeff_lower, place_lower)
    upper_terms = sibling_terms(coeff_upper, place_upper)
    all_coeffs = coeff_top.transpose(1, 0, 2).reshape(COLUMNS, TOPS * RANK)
    all_places = place_top.transpose(1, 0, 2).reshape(DIMS, TOPS * RANK)
    owner = jnp.arange(TOPS * RANK, dtype=jnp.int32) // RANK

    def top_one(pair):
        node, place = pair
        masked = jnp.where((owner != node)[None, :], all_coeffs, 0.0)
        return jnp.dot(masked, kernel_block(all_places, place), precision=HIGH, preferred_element_type=jnp.float32)

    top_terms = lax.map(top_one, (jnp.arange(TOPS, dtype=jnp.int32), place_top))
    upper_full = descend(top_terms, transfer_upper, upper_terms)
    lower_full = descend(upper_full, transfer_lower, lower_terms)
    leaf_full = descend(lower_full, transfer_leaf, leaf_terms).astype(jnp.bfloat16)

    def leaf_out(items):
        near_part, expansion, generator = items
        far = jnp.dot(expansion, generator.T, preferred_element_type=jnp.float32)
        return (near_part.astype(jnp.float32) + far).astype(jnp.bfloat16)

    result = lax.map(leaf_out, (near, leaf_full, basis))
    return result.transpose(1, 0, 2).reshape(COLUMNS, POINTS)
```

```python
import jax
import jax.numpy as jnp
from jax import lax
from jax.experimental import pallas as pl
from jax.experimental.pallas import tpu as pltpu
from jax.sharding import PartitionSpec as P

RIDGE = 1.0
SCALE = (2.0 * 1.4426950408889634) ** 0.5
BF = jnp.bfloat16
F32 = jnp.float32
VMEM_LIMIT = 64 * 1024 * 1024 - 131072


def mm(a, b):
    return jnp.dot(a, b, preferred_element_type=F32)


def mm_nt(a, b):
    return lax.dot_general(a, b, (((1,), (1,)), ((), ())), preferred_element_type=F32)


def mm_tn(a, b):
    return lax.dot_general(a, b, (((0,), (0,)), ((), ())), preferred_element_type=F32)


def halves(x):
    hi = x.astype(BF)
    return hi, (x - hi.astype(F32)).astype(BF)


def stacked(x):
    return jnp.concatenate(halves(x), axis=0)


def fold(x):
    rows = x.shape[0] // 2
    return x[:rows] + x[rows:]


def chosen(index, count):
    rows = lax.broadcasted_iota(jnp.int32, (count, index.shape[1]), 0)
    return jnp.where(rows == index, 1.0, 0.0).astype(BF)


def operands(h, m):
    full = h.astype(F32) + m.astype(F32)
    norm = -0.5 * jnp.sum(full * full, axis=0, keepdims=True)
    n1 = norm.astype(BF).astype(F32)
    n2 = (norm - n1).astype(BF).astype(F32)
    n3 = norm - n1 - n2
    row = lax.broadcasted_iota(jnp.int32, (16, h.shape[1]), 0)
    one = jnp.where((row >= 3) & (row < 6), 1.0, 0.0)
    left = jnp.where(row == 0, n1, jnp.where(row == 1, n2, jnp.where(row == 2, n3, one)))
    one = jnp.where(row < 3, 1.0, 0.0)
    right = jnp.where(row == 3, n1, jnp.where(row == 4, n2, jnp.where(row == 5, n3, one)))
    return (
        jnp.concatenate([h, h, m, left.astype(BF)], axis=0),
        jnp.concatenate([h, m, h, right.astype(BF)], axis=0),
    )


def up_kernel(
    rhs, pts, basis, idx_leaf, idx_lower, idx_upper, t_leaf, t_lower, t_upper,
    c0_out, s0_out, c1_out, s1_out, msg_out, c1_all, s1_all,
):
    step = pl.program_id(0)
    coeffs, places = [], []
    for q in range(4):
        cols = slice(512 * q, 512 * (q + 1))
        coeffs.append(mm(rhs[:, cols], basis[q]))
        hm = stacked(pts[:, cols] * SCALE)
        pick = chosen(idx_leaf[pl.ds(4 * step + q, 1), :], 512)
        places.append(mm(hm, pick).astype(BF))
    c0 = jnp.concatenate(coeffs, axis=1)
    s0 = jnp.concatenate(places, axis=1)
    c0_out[...] = c0
    s0_out[...] = s0
    c1 = fold(mm(stacked(c0), t_leaf[...].reshape(512, 128)))
    s1 = mm(s0, chosen(idx_lower[pl.ds(step, 1), :], 512)).astype(BF)
    c1_out[...] = c1
    s1_out[...] = s1
    lanes = pl.ds(pl.multiple_of(step * 128, 128), 128)
    c1_all[:, lanes] = c1
    s1_all[:, lanes] = s1

    @pl.when(step == 3)
    def _():
        c2 = fold(mm(stacked(c1_all[...]), t_lower[...].reshape(512, 128)))
        s2 = mm(s1_all[...], chosen(idx_upper[...], 512)).astype(BF)
        raised = fold(mm(stacked(c2), t_upper[0]))
        msg = jnp.concatenate([c2.astype(BF), stacked(raised), s2], axis=0)
        for k in range(4):
            msg_out[k] = msg


def mid_kernel(got, idx_top, msg_out, place_out, turned):
    position = lax.axis_index("leaf")
    c3 = jnp.zeros((32, 128), F32)
    for k in range(4):
        c3 = c3 + got[k, 32:64, :].astype(F32) + got[k, 64:96, :].astype(F32)
    s2 = jnp.concatenate([got[k, 96:160, :] for k in range(4)], axis=1)
    s3 = mm(s2, chosen(idx_top[pl.ds(position // 4, 1), :], 512))
    place_out[...] = s3.astype(BF)
    hi, lo = halves(c3)
    rows = jnp.concatenate([hi.astype(F32), lo.astype(F32), s3], axis=0)
    turned[...] = rows.T
    quarter = pl.ds(pl.multiple_of((position % 4) * 32, 32), 32)
    msg = turned[quarter, :].astype(BF)
    for k in range(32):
        msg_out[k] = msg


def sibling_sum(c, left, right):
    chl = stacked(c)
    total = []
    for t in range(4):
        out = slice(128 * t, 128 * (t + 1))
        acc = jnp.zeros((32, 128), F32)
        for s in range(4):
            if s == t:
                continue
            src = slice(128 * s, 128 * (s + 1))
            block = jnp.exp2(mm_tn(left[:, src], right[:, out]))
            hi, lo = halves(block)
            acc = acc + fold(mm(chl[:, src], hi)) + mm(chl[:32, src], lo)
        total.append(acc)
    return jnp.concatenate(total, axis=1)


def near_kernel(
    rhs, pts, c0, s0, c1, s1, got, place3,
    near_out, t0_out, t1_out, t2_out,
):
    step = pl.program_id(0)
    for q in range(4):
        base = 512 * q
        x = rhs[:, base:base + 512]
        h, m = halves(pts[:, base:base + 512] * SCALE)
        left, right = operands(h, m)
        for t in range(2):
            out = slice(256 * t, 256 * (t + 1))
            acc = x[:, out].astype(F32) * RIDGE
            total = jnp.zeros((32, 256), F32)
            for s in range(2):
                src = slice(256 * s, 256 * (s + 1))
                block = jnp.exp2(mm_tn(left[:, src], right[:, out])).astype(BF)
                total = total + mm(x[:, src], block)
            near_out[:, base + 256 * t:base + 256 * (t + 1)] = (total + acc).astype(BF)
    t0_out[...] = sibling_sum(c0[...], *operands(s0[:32, :], s0[32:, :]))

    @pl.when(step == 3)
    def _():
        t1_out[...] = sibling_sum(c1[...], *operands(s1[:32, :], s1[32:, :]))
        mine = lax.axis_index("leaf") % 4
        target, _ = operands(got[mine, 96:128, :], got[mine, 128:160, :])
        acc = jnp.zeros((32, 128), F32)
        for k in range(4):
            _, source = operands(got[k, 96:128, :], got[k, 128:160, :])
            block = jnp.exp2(mm_tn(target, source))
            hi, lo = halves(block)
            c2 = jnp.where(mine == k, 0.0, got[k, 0:32, :].astype(F32)).astype(BF)
            acc = acc + mm_nt(c2, hi) + mm_nt(c2, lo)
        t2_out[...] = acc


def top_kernel(got, place3, t2, out):
    node = lax.axis_index("leaf") // 4
    turned = got[...].reshape(1024, 128).T
    column = lax.broadcasted_iota(jnp.int32, (64, 1024), 1)
    c3 = jnp.where(column // 32 == node, 0.0, turned[:64].astype(F32)).astype(BF)
    target, _ = operands(place3[:32, :], place3[32:, :])
    _, source = operands(turned[64:96], turned[96:])
    acc = jnp.zeros((32, 128), F32)
    for k in range(4):
        cols = slice(256 * k, 256 * (k + 1))
        hi, lo = halves(jnp.exp2(mm_tn(target, source[:, cols])))
        acc = acc + fold(mm_nt(c3[:, cols], hi)) + mm_nt(c3[:32, cols], lo)
    for k in range(4):
        out[k] = acc


def down_kernel(
    got, t0, t1, t2, near, basis, t_leaf, t_lower, t_upper,
    out, g1_all,
):
    step = pl.program_id(0)

    @pl.when(step == 0)
    def _():
        t3 = (got[0] + got[1]) + (got[2] + got[3])
        g2 = t2[...] + fold(mm_nt(stacked(t3), t_upper[0]))
        g1_all[...] = t1[...] + fold(mm_nt(stacked(g2), t_lower[...].reshape(512, 128)))

    g1 = g1_all[:, pl.ds(pl.multiple_of(step * 128, 128), 128)]
    g0 = t0[...] + fold(mm_nt(stacked(g1), t_leaf[...].reshape(512, 128)))
    g0 = g0.astype(BF)
    for q in range(4):
        cols = slice(512 * q, 512 * (q + 1))
        far = mm_nt(g0[:, 128 * q:128 * (q + 1)], basis[q])
        out[:, cols] = (near[:, cols].astype(F32) + far).astype(BF)


def whole(shape):
    return pl.BlockSpec(shape, lambda i: (0,) * len(shape))


def params():
    return pltpu.CompilerParams(vmem_limit_bytes=VMEM_LIMIT)


def per_device(
    rhs_block, points, basis, skeleton_leaf, skeleton_lower, skeleton_upper,
    skeleton_top, transfer_leaf, transfer_lower, transfer_upper,
):
    shape = jax.ShapeDtypeStruct
    wide = pl.BlockSpec((32, 2048), lambda i: (0, i))
    leaf_basis = pl.BlockSpec((4, 512, 128), lambda i: (i, 0, 0))
    leaf_transfer = pl.BlockSpec((4, 128, 128), lambda i: (i, 0, 0))

    c0, s0, c1, s1, msg1 = pl.pallas_call(
        up_kernel,
        grid=(4,),
        in_specs=[
            wide, wide, leaf_basis,
            whole((16, 128)), whole((4, 128)), whole((1, 128)),
            leaf_transfer, whole((4, 128, 128)), whole((1, 128, 128)),
        ],
        out_specs=[
            pl.BlockSpec((32, 512), lambda i: (0, i)),
            pl.BlockSpec((64, 512), lambda i: (0, i)),
            pl.BlockSpec((32, 128), lambda i: (0, i)),
            pl.BlockSpec((64, 128), lambda i: (0, i)),
            whole((4, 160, 128)),
        ],
        out_shape=[
            shape((32, 2048), F32), shape((64, 2048), BF),
            shape((32, 512), F32), shape((64, 512), BF),
            shape((4, 160, 128), BF),
        ],
        scratch_shapes=[pltpu.VMEM((32, 512), F32), pltpu.VMEM((64, 512), BF)],
        compiler_params=params(),
        cost_estimate=pl.CostEstimate(flops=10**9, bytes_accessed=5 * 10**6, transcendentals=0),
        name="upward",
    )(rhs_block, points, basis, skeleton_leaf, skeleton_lower, skeleton_upper,
      transfer_leaf, transfer_lower, transfer_upper)

    nodes = lax.axis_size("leaf") // 4
    siblings = [[4 * k + i for i in range(4)] for k in range(nodes)]
    same_place = [[4 * k + i for k in range(nodes)] for i in range(4)]
    got1 = lax.all_to_all(msg1, "leaf", 0, 0, axis_index_groups=siblings, tiled=True)

    msg2, place3 = pl.pallas_call(
        mid_kernel,
        out_shape=[shape((32, 32, 128), BF), shape((64, 128), BF)],
        scratch_shapes=[pltpu.VMEM((128, 128), F32)],
        compiler_params=params(),
        name="middle",
    )(got1, skeleton_top)

    got2 = lax.all_to_all(msg2, "leaf", 0, 0, axis_index_groups=same_place, tiled=True)

    near, t0, t1, t2 = pl.pallas_call(
        near_kernel,
        grid=(4,),
        in_specs=[
            wide, wide,
            pl.BlockSpec((32, 512), lambda i: (0, i)),
            pl.BlockSpec((64, 512), lambda i: (0, i)),
            whole((32, 512)), whole((64, 512)), whole((4, 160, 128)),
            pl.BlockSpec(memory_space=pl.ANY),
        ],
        out_specs=[
            wide, pl.BlockSpec((32, 512), lambda i: (0, i)),
            whole((32, 512)), whole((32, 128)),
        ],
        out_shape=[
            shape((32, 8192), BF), shape((32, 2048), F32),
            shape((32, 512), F32), shape((32, 128), F32),
        ],
        compiler_params=params(),
        cost_estimate=pl.CostEstimate(
            flops=6 * 10**9, bytes_accessed=3 * 10**6, transcendentals=5 * 10**6),
        name="near",
    )(rhs_block, points, c0, s0, c1, s1, got1, place3)

    part = pl.pallas_call(
        top_kernel,
        in_specs=[whole((32, 32, 128)), whole((64, 128)), pl.BlockSpec(memory_space=pl.ANY)],
        out_specs=whole((4, 32, 128)),
        grid=(1,),
        out_shape=shape((4, 32, 128), F32),
        compiler_params=params(),
        name="top",
    )(got2, place3, t2)

    got3 = lax.all_to_all(part, "leaf", 0, 0, axis_index_groups=siblings, tiled=True)

    return pl.pallas_call(
        down_kernel,
        grid=(4,),
        in_specs=[
            whole((4, 32, 128)),
            pl.BlockSpec((32, 512), lambda i: (0, i)),
            whole((32, 512)), whole((32, 128)), wide, leaf_basis,
            leaf_transfer, whole((4, 128, 128)), whole((1, 128, 128)),
        ],
        out_specs=wide,
        out_shape=shape((32, 8192), BF),
        scratch_shapes=[pltpu.VMEM((32, 512), F32)],
        compiler_params=params(),
        cost_estimate=pl.CostEstimate(
            flops=2 * 10**9, bytes_accessed=5 * 10**6, transcendentals=10**6),
        name="downward",
    )(got3, t0, t1, t2, near, basis, transfer_leaf,
      transfer_lower, transfer_upper)


def solution(mesh):
    return jax.shard_map(
        per_device,
        mesh=mesh,
        in_specs=(
            P("rhs", "leaf"),
            P(None, "leaf"),
            P("leaf", None, None),
            P("leaf", None),
            P("leaf", None),
            P("leaf", None),
            P(),
            P("leaf", None, None),
            P("leaf", None, None),
            P("leaf", None, None),
        ),
        out_specs=P("rhs", "leaf"),
        check_vma=False,
    )
```

```python
import jax
import jax.numpy as jnp
from jax import lax
from jax.experimental import pallas as pl
from jax.experimental.pallas import tpu as pltpu
from jax.sharding import PartitionSpec as P

RIDGE = 1.0
SCALE = (2.0 * 1.4426950408889634) ** 0.5
BF = jnp.bfloat16
F32 = jnp.float32
VMEM_LIMIT = 32 * 1024 * 1024


def mm(a, b):
    return jnp.dot(a, b, preferred_element_type=F32)


def mm_nt(a, b):
    return lax.dot_general(a, b, (((1,), (1,)), ((), ())), preferred_element_type=F32)


def mm_tn(a, b):
    return lax.dot_general(a, b, (((0,), (0,)), ((), ())), preferred_element_type=F32)


def halves(x):
    hi = x.astype(BF)
    return hi, (x - hi.astype(F32)).astype(BF)


def stacked(x):
    return jnp.concatenate(halves(x), axis=0)


def fold(x):
    rows = x.shape[0] // 2
    return x[:rows] + x[rows:]


def chosen(index, count):
    rows = lax.broadcasted_iota(jnp.int32, (count, index.shape[1]), 0)
    return jnp.where(rows == index, 1.0, 0.0).astype(BF)


def operands(h, m):
    full = h.astype(F32) + m.astype(F32)
    norm = -0.5 * jnp.sum(full * full, axis=0, keepdims=True)
    n1 = norm.astype(BF).astype(F32)
    n2 = (norm - n1).astype(BF).astype(F32)
    n3 = norm - n1 - n2
    row = lax.broadcasted_iota(jnp.int32, (16, h.shape[1]), 0)
    one = jnp.where((row >= 3) & (row < 6), 1.0, 0.0)
    left = jnp.where(row == 0, n1, jnp.where(row == 1, n2, jnp.where(row == 2, n3, one)))
    one = jnp.where(row < 3, 1.0, 0.0)
    right = jnp.where(row == 3, n1, jnp.where(row == 4, n2, jnp.where(row == 5, n3, one)))
    return (
        jnp.concatenate([h, h, m, left.astype(BF)], axis=0),
        jnp.concatenate([h, m, h, right.astype(BF)], axis=0),
    )


def copies(pairs, sems, start=0):
    return [
        pltpu.make_async_copy(src, dst, sems.at[start + k])
        for k, (src, dst) in enumerate(pairs)
    ]


def up_kernel(
    rhs, pts, basis, idx_leaf, idx_lower, idx_upper, idx_top, t_leaf, t_lower, t_upper,
    it_v, c0_v, s0_v, c1_v, s1_v, msg_v,
    rhs_v, pts_v, basis_v, tl_v, tlo_v, tu_v, il_v, ilo_v, iu_v, sems, chunk_sems,
):
    small = copies(
        [
            (idx_leaf, il_v), (idx_lower, ilo_v), (idx_upper, iu_v), (t_lower, tlo_v),
            (t_upper, tu_v), (idx_top, it_v),
        ], sems)

    def arrivals(step):
        cols = pl.ds(pl.multiple_of(step * 2048, 2048), 2048)
        leaves = pl.ds(step * 4, 4)
        return copies(
            [
                (pts.at[:, cols], pts_v.at[step]), (rhs.at[:, cols], rhs_v.at[step]),
                (basis.at[leaves], basis_v.at[step]), (t_leaf.at[leaves], tl_v.at[step]),
            ], chunk_sems, 4 * step)

    small[0].start()
    for step in range(4):
        for copy in arrivals(step):
            copy.start()
        if step == 0:
            for copy in small[1:]:
                copy.start()
    small[0].wait()
    small[1].wait()

    def chunk(step, carry):
        for copy in arrivals(step):
            copy.wait()
        coeffs, places = [], []
        for q in range(4):
            cols = slice(512 * q, 512 * (q + 1))
            coeffs.append(mm(rhs_v[step, :, cols], basis_v[step, q]))
            hm = stacked(pts_v[step, :, cols] * SCALE)
            pick = chosen(il_v[pl.ds(4 * step + q, 1), :], 512)
            places.append(mm(hm, pick).astype(BF))
        c0 = jnp.concatenate(coeffs, axis=1)
        s0 = jnp.concatenate(places, axis=1)
        c0_v[step] = c0
        s0_v[step] = s0
        c1 = fold(mm(stacked(c0), tl_v[step].reshape(512, 128)))
        s1 = mm(s0, chosen(ilo_v[pl.ds(step, 1), :], 512)).astype(BF)
        lanes = pl.ds(pl.multiple_of(step * 128, 128), 128)
        c1_v[:, lanes] = c1
        s1_v[:, lanes] = s1
        return carry

    lax.fori_loop(0, 4, chunk, 0)
    for copy in small[2:]:
        copy.wait()
    c2 = fold(mm(stacked(c1_v[...]), tlo_v[...].reshape(512, 128)))
    s2 = mm(s1_v[...], chosen(iu_v[...], 512)).astype(BF)
    raised = fold(mm(stacked(c2), tu_v[0]))
    msg = jnp.concatenate([c2.astype(BF), stacked(raised), s2], axis=0)
    for k in range(4):
        msg_v[k] = msg


def mid_kernel(got, idx_top, msg_out, place_out):
    position = lax.axis_index("leaf")
    c3 = jnp.zeros((32, 128), F32)
    for k in range(4):
        c3 = c3 + got[k, 32:64, :].astype(F32) + got[k, 64:96, :].astype(F32)
    s2 = jnp.concatenate([got[k, 96:160, :] for k in range(4)], axis=1)
    s3 = mm(s2, chosen(idx_top[pl.ds(position // 4, 1), :], 512))
    place_out[...] = s3.astype(BF)
    rows = jnp.concatenate([c3, s3], axis=0)
    moved = pltpu.roll(rows, 64, 1)
    low = lax.broadcasted_iota(jnp.int32, (48, 128), 1) < 64
    first = position % 2 == 0
    msg = jnp.where(
        low,
        jnp.where(first, rows[:48], moved[:48]),
        jnp.where(first, moved[48:], rows[48:]),
    ).astype(BF)
    for k in range(32):
        msg_out[k] = msg


def sibling_sum(c, left, right):
    chl = stacked(c)
    block = jnp.exp2(mm_tn(left, right))
    zero = jnp.zeros((128, 128), F32)
    rows = []
    for s in range(4):
        src = slice(128 * s, 128 * (s + 1))
        rows.append(jnp.concatenate(
            [zero if s == t else block[src, 128 * t:128 * (t + 1)] for t in range(4)], axis=1))
    hi, lo = halves(jnp.concatenate(rows, axis=0))
    return fold(mm(chl, hi)) + mm(chl[:32], lo)


def near_kernel(
    rhs, pts, basis, t_lower, t_upper, c0, s0, c1, s1, got, place3,
    near_out, t0_out, t1_out, t2_out, basis_out, above_out,
    rhs_v, pts_v, near_v, t0_v, sems, chunk_sems, out_sems,
):
    ahead = copies(
        [
            (basis, basis_out), (t_lower, above_out.at[pl.ds(0, 4)]),
            (t_upper, above_out.at[pl.ds(4, 1)]),
        ], sems)

    def arrivals(step):
        cols = pl.ds(pl.multiple_of(step * 2048, 2048), 2048)
        return copies(
            [(pts.at[:, cols], pts_v.at[step]), (rhs.at[:, cols], rhs_v.at[step])],
            chunk_sems, 2 * step)

    def departures(step):
        return copies(
            [(near_v.at[step], near_out.at[step]), (t0_v.at[step], t0_out.at[step])],
            out_sems, 2 * step)

    for step in range(4):
        for copy in arrivals(step):
            copy.start()
    for copy in ahead:
        copy.start()

    def chunk(step, carry):
        for copy in arrivals(step):
            copy.wait()
        for q in range(4):
            leaf = slice(512 * q, 512 * (q + 1))
            x = rhs_v[step, :, leaf]
            left, right = operands(*halves(pts_v[step, :, leaf] * SCALE))
            wide = jnp.exp2(mm_tn(left[:, :256], right)).astype(BF)
            last = jnp.exp2(mm_tn(left[:, 256:], right[:, 256:])).astype(BF)
            both = mm(x[:, :256], wide) + RIDGE * x.astype(F32)
            first = both[:, :256] + mm_nt(x[:, 256:], wide[:, 256:])
            second = both[:, 256:] + mm(x[:, 256:], last)
            near_v[step, :, leaf] = jnp.concatenate([first, second], axis=1).astype(BF)
        t0_v[step] = sibling_sum(c0[step], *operands(s0[step, :32, :], s0[step, 32:, :]))
        for copy in departures(step):
            copy.start()
        return carry

    lax.fori_loop(0, 4, chunk, 0)
    t1_out[...] = sibling_sum(c1[...], *operands(s1[:32, :], s1[32:, :]))
    mine = lax.axis_index("leaf") % 4
    target, _ = operands(got[mine, 96:128, :], got[mine, 128:160, :])

    def side(rows):
        return jnp.concatenate([got[k, rows, :] for k in range(4)], axis=1)

    _, source = operands(side(slice(96, 128)), side(slice(128, 160)))
    hi, lo = halves(jnp.exp2(mm_tn(target, source)))
    c2 = jnp.concatenate(
        [jnp.where(mine == k, 0.0, got[k, 0:32, :].astype(F32)) for k in range(4)], axis=1
    ).astype(BF)
    t2_out[...] = mm_nt(c2, hi) + mm_nt(c2, lo)
    for copy in ahead:
        copy.wait()
    for step in range(4):
        for copy in departures(step):
            copy.wait()


def top_kernel(got, place3, t2, out):
    node = lax.axis_index("leaf") // 4
    target, _ = operands(place3[:32, :], place3[32:, :])
    low = lax.broadcasted_iota(jnp.int32, (48, 128), 1) < 64
    column = lax.broadcasted_iota(jnp.int32, (32, 512), 1)
    acc = jnp.zeros((32, 128), F32)
    for first in range(0, 32, 8):
        parts = []
        for k in range(first, first + 8, 2):
            even, odd = got[k].astype(F32), got[k + 1].astype(F32)
            parts.append(jnp.concatenate([
                jnp.where(low, even, pltpu.roll(odd, 64, 1)),
                jnp.where(low, pltpu.roll(even, 64, 1), odd),
            ], axis=0))
        rows = jnp.concatenate(parts, axis=1)
        c3 = jnp.where(column // 64 == node - first, 0.0, rows[:32]).astype(BF)
        _, source = operands(rows[32:64].astype(BF), rows[64:].astype(BF))
        hi, lo = halves(jnp.exp2(mm_tn(target, source)))
        acc = acc + mm_nt(c3, hi) + mm_nt(c3, lo)
    out[...] = acc


def down_kernel(
    part, other, t0, t1, t2, near, basis, t_leaf, above,
    out, near_v, t0_v, tl_v, out_v, in_sems, out_sems,
):
    arrivals = copies(
        [(t0, t0_v), (t_leaf, tl_v)] + [(near.at[k], near_v.at[k]) for k in range(4)], in_sems)
    for copy in arrivals:
        copy.start()

    def departure(step):
        cols = pl.ds(pl.multiple_of(step * 2048, 2048), 2048)
        return pltpu.make_async_copy(out_v.at[step], out.at[:, cols], out_sems.at[step])

    t3 = part[...] + other[...]
    g2 = t2[...] + fold(mm_nt(stacked(t3), above[4]))
    g1 = t1[...] + fold(mm_nt(stacked(g2), above[:4].reshape(512, 128)))
    for copy in arrivals[:2]:
        copy.wait()
    g0 = []
    for step in range(4):
        here = stacked(g1[:, 128 * step:128 * (step + 1)])
        g0.append((t0_v[step] + fold(mm_nt(here, tl_v[4 * step:4 * step + 4].reshape(512, 128)))).astype(BF))
    for step in range(4):
        arrivals[2 + step].wait()
        for q in range(4):
            cols = slice(512 * q, 512 * (q + 1))
            far = mm_nt(g0[step][:, 128 * q:128 * (q + 1)], basis[4 * step + q])
            out_v[step, :, cols] = (near_v[step, :, cols].astype(F32) + far).astype(BF)
        departure(step).start()
    for step in range(4):
        departure(step).wait()


def call(kernel, name, ins, outs, scratch=(), cost=None, **kwargs):
    spec = lambda space: pl.BlockSpec(memory_space=space)
    return pl.pallas_call(
        kernel,
        in_specs=[spec(space) for _, space in ins],
        out_specs=[spec(space) for _, _, space in outs],
        out_shape=[
            (space if space is not pl.ANY else jax.ShapeDtypeStruct)(shape, dtype)
            for shape, dtype, space in outs
        ],
        scratch_shapes=list(scratch),
        compiler_params=pltpu.CompilerParams(vmem_limit_bytes=VMEM_LIMIT),
        cost_estimate=cost,
        name=name,
    )(*[pltpu.with_memory_space_constraint(x, space) for x, space in ins])


def per_device(
    rhs_block, points, basis, skeleton_leaf, skeleton_lower, skeleton_upper,
    skeleton_top, transfer_leaf, transfer_lower, transfer_upper,
):
    vmem, hbm, dma = pltpu.VMEM, pltpu.HBM, pltpu.SemaphoreType.DMA
    i32 = jnp.int32

    def inside(*arrays):
        return [(x, vmem) for x in arrays]

    def outside(*arrays):
        return [(x, hbm) for x in arrays]

    transfers = (transfer_leaf, transfer_lower, transfer_upper)
    top_index, c0, s0, c1, s1, msg1 = call(
        up_kernel, "upward",
        outside(
            rhs_block, points, basis, skeleton_leaf, skeleton_lower, skeleton_upper,
            skeleton_top, *transfers),
        [
            ((32, 128), i32, vmem), ((4, 32, 512), F32, vmem), ((4, 64, 512), BF, vmem),
            ((32, 512), F32, vmem), ((64, 512), BF, vmem), ((4, 160, 128), BF, vmem),
        ],
        [
            vmem((4, 32, 2048), BF), vmem((4, 32, 2048), F32), vmem((4, 4, 512, 128), BF),
            vmem((4, 4, 128, 128), BF), vmem((4, 128, 128), BF), vmem((1, 128, 128), BF),
            vmem((16, 128), i32), vmem((4, 128), i32), vmem((1, 128), i32),
            dma((6,)), dma((16,)),
        ],
        pl.CostEstimate(flops=10**9, bytes_accessed=5 * 10**6, transcendentals=0),
    )

    nodes = lax.axis_size("leaf") // 4
    siblings = [[4 * k + i for i in range(4)] for k in range(nodes)]
    turn = (0, 0, 1, 1)
    across = [
        [4 * k + 2 * (turn[k % 4] ^ chip) + core for k in range(nodes)]
        for chip in range(2) for core in range(2)
    ]
    got1 = lax.all_to_all(msg1, "leaf", 0, 0, axis_index_groups=siblings, tiled=True)

    msg2, place3 = call(
        mid_kernel, "middle", inside(got1, top_index),
        [((32, 48, 128), BF, vmem), ((64, 128), BF, vmem)],
    )

    got2 = lax.all_to_all(msg2, "leaf", 0, 0, axis_index_groups=across, tiled=True)

    near, t0, t1, t2, gens, above = call(
        near_kernel, "near",
        outside(rhs_block, points, basis, transfer_lower, transfer_upper)
        + inside(c0, s0, c1, s1, got1, place3),
        [
            ((4, 32, 2048), BF, hbm), ((4, 32, 512), F32, hbm),
            ((32, 512), F32, vmem), ((32, 128), F32, vmem),
            ((16, 512, 128), BF, vmem), ((5, 128, 128), BF, vmem),
        ],
        [
            vmem((4, 32, 2048), BF), vmem((4, 32, 2048), F32), vmem((4, 32, 2048), BF),
            vmem((4, 32, 512), F32), dma((3,)), dma((8,)), dma((8,)),
        ],
        pl.CostEstimate(flops=6 * 10**9, bytes_accessed=3 * 10**6, transcendentals=5 * 10**6),
    )

    part, = call(
        top_kernel, "top", inside(got2, place3, t2), [((32, 128), F32, vmem)])

    partner = [(i, i ^ 1) for i in range(4 * nodes)]
    other = lax.ppermute(part, "leaf", partner)

    product, = call(
        down_kernel, "downward",
        inside(part, other) + outside(t0) + inside(t1, t2) + outside(near)
        + inside(gens) + outside(transfer_leaf) + inside(above),
        [((32, 8192), BF, hbm)],
        [
            vmem((4, 32, 2048), BF), vmem((4, 32, 512), F32), vmem((16, 128, 128), BF),
            vmem((4, 32, 2048), BF), dma((6,)), dma((4,)),
        ],
        pl.CostEstimate(flops=2 * 10**9, bytes_accessed=5 * 10**6, transcendentals=10**6),
    )
    return product


def solution(mesh):
    return jax.shard_map(
        per_device,
        mesh=mesh,
        in_specs=(
            P("rhs", "leaf"),
            P(None, "leaf"),
            P("leaf", None, None),
            P("leaf", None),
            P("leaf", None),
            P("leaf", None),
            P(),
            P("leaf", None, None),
            P("leaf", None, None),
            P("leaf", None, None),
        ),
        out_specs=P("rhs", "leaf"),
        check_vma=False,
    )
```

```python
import jax
import jax.numpy as jnp
from jax import lax
from jax.experimental import pallas as pl
from jax.experimental.pallas import tpu as pltpu
from jax.sharding import PartitionSpec as P

RIDGE = 1.0
SCALE = (2.0 * 1.4426950408889634) ** 0.5
BF = jnp.bfloat16
F32 = jnp.float32
VMEM_LIMIT = 32 * 1024 * 1024


def mm(a, b):
    return jnp.dot(a, b, preferred_element_type=F32)


def mm_nt(a, b):
    return lax.dot_general(a, b, (((1,), (1,)), ((), ())), preferred_element_type=F32)


def mm_tn(a, b):
    return lax.dot_general(a, b, (((0,), (0,)), ((), ())), preferred_element_type=F32)


def halves(x):
    hi = x.astype(BF)
    return hi, (x - hi.astype(F32)).astype(BF)


def stacked(x):
    return jnp.concatenate(halves(x), axis=0)


def fold(x):
    rows = x.shape[0] // 2
    return x[:rows] + x[rows:]


def chosen(index, count):
    rows = lax.broadcasted_iota(jnp.int32, (count, index.shape[1]), 0)
    return jnp.where(rows == index, 1.0, 0.0).astype(BF)


def operands(h, m):
    full = h.astype(F32) + m.astype(F32)
    norm = -0.5 * jnp.sum(full * full, axis=0, keepdims=True)
    n1 = norm.astype(BF).astype(F32)
    n2 = (norm - n1).astype(BF).astype(F32)
    n3 = norm - n1 - n2
    row = lax.broadcasted_iota(jnp.int32, (16, h.shape[1]), 0)
    one = jnp.where((row >= 3) & (row < 6), 1.0, 0.0)
    left = jnp.where(row == 0, n1, jnp.where(row == 1, n2, jnp.where(row == 2, n3, one)))
    one = jnp.where(row < 3, 1.0, 0.0)
    right = jnp.where(row == 3, n1, jnp.where(row == 4, n2, jnp.where(row == 5, n3, one)))
    return (
        jnp.concatenate([h, h, m, left.astype(BF)], axis=0),
        jnp.concatenate([h, m, h, right.astype(BF)], axis=0),
    )


def copies(pairs, sems, start=0):
    return [
        pltpu.make_async_copy(src, dst, sems.at[start + k])
        for k, (src, dst) in enumerate(pairs)
    ]


def up_kernel(
    rhs, pts, basis, idx_leaf, idx_lower, idx_upper, idx_top, t_leaf, t_lower, t_upper,
    it_v, c0_out, s0_out, c1_v, s1_v, msg_v,
    rhs_v, pts_v, basis_v, tl_v, tlo_v, tu_v, il_v, ilo_v, iu_v,
    c0_v, s0_v, sems, chunk_sems, out_sems,
):
    small = copies(
        [
            (idx_leaf, il_v), (idx_lower, ilo_v), (idx_upper, iu_v), (t_lower, tlo_v),
            (t_upper, tu_v), (idx_top, it_v),
        ], sems)

    def arrivals(step):
        cols = pl.ds(pl.multiple_of(step * 2048, 2048), 2048)
        leaves = pl.ds(step * 4, 4)
        return copies(
            [
                (pts.at[:, cols], pts_v.at[step]), (rhs.at[:, cols], rhs_v.at[step]),
                (basis.at[leaves], basis_v.at[step]), (t_leaf.at[leaves], tl_v.at[step]),
            ], chunk_sems, 4 * step)

    def departures(step):
        return copies(
            [(c0_v.at[step], c0_out.at[step]), (s0_v.at[step], s0_out.at[step])],
            out_sems, 2 * step)

    small[0].start()
    for step in range(4):
        for copy in arrivals(step):
            copy.start()
        if step == 0:
            for copy in small[1:]:
                copy.start()
    small[0].wait()
    small[1].wait()

    def chunk(step, carry):
        for copy in arrivals(step):
            copy.wait()
        coeffs, places = [], []
        for q in range(4):
            cols = slice(512 * q, 512 * (q + 1))
            coeffs.append(mm(rhs_v[step, :, cols], basis_v[step, q]))
            hm = stacked(pts_v[step, :, cols] * SCALE)
            pick = chosen(il_v[pl.ds(4 * step + q, 1), :], 512)
            places.append(mm(hm, pick).astype(BF))
        c0 = jnp.concatenate(coeffs, axis=1)
        s0 = jnp.concatenate(places, axis=1)
        c0_v[step] = c0
        s0_v[step] = s0
        for copy in departures(step):
            copy.start()
        return carry

    lax.fori_loop(0, 4, chunk, 0)
    for n in range(4):
        lanes = slice(128 * n, 128 * (n + 1))
        c1_v[:, lanes] = fold(mm(stacked(c0_v[n]), tl_v[n].reshape(512, 128)))
        s1_v[:, lanes] = mm(s0_v[n], chosen(ilo_v[n:n + 1, :], 512)).astype(BF)
    for copy in small[2:]:
        copy.wait()
    c2 = fold(mm(stacked(c1_v[...]), tlo_v[...].reshape(512, 128)))
    s2 = mm(s1_v[...], chosen(iu_v[...], 512)).astype(BF)
    raised = fold(mm(stacked(c2), tu_v[0]))
    msg = jnp.concatenate([c2.astype(BF), stacked(raised), s2], axis=0)
    for k in range(4):
        msg_v[k] = msg
    for step in range(4):
        for copy in departures(step):
            copy.wait()


def mid_kernel(got, idx_top, msg_out, place_out):
    position = lax.axis_index("leaf")
    c3 = jnp.zeros((32, 128), F32)
    for k in range(4):
        c3 = c3 + got[k, 32:64, :].astype(F32) + got[k, 64:96, :].astype(F32)
    s2 = jnp.concatenate([got[k, 96:160, :] for k in range(4)], axis=1)
    s3 = mm(s2, chosen(idx_top[pl.ds(position // 4, 1), :], 512))
    place_out[...] = s3.astype(BF)
    rows = jnp.concatenate([c3, s3], axis=0)
    moved = pltpu.roll(rows, 64, 1)
    low = lax.broadcasted_iota(jnp.int32, (48, 128), 1) < 64
    first = position % 2 == 0
    msg = jnp.where(
        low,
        jnp.where(first, rows[:48], moved[:48]),
        jnp.where(first, moved[48:], rows[48:]),
    ).astype(BF)
    for k in range(32):
        msg_out[k] = msg


def sibling_sum(c, left, right):
    chl = stacked(c)
    block = jnp.exp2(mm_tn(left, right))
    zero = jnp.zeros((128, 128), F32)
    rows = []
    for s in range(4):
        src = slice(128 * s, 128 * (s + 1))
        rows.append(jnp.concatenate(
            [zero if s == t else block[src, 128 * t:128 * (t + 1)] for t in range(4)], axis=1))
    hi, lo = halves(jnp.concatenate(rows, axis=0))
    return fold(mm(chl, hi)) + mm(chl[:32], lo)


def near_kernel(
    rhs, pts, basis, t_lower, t_upper, c0, s0, c1, s1, got, place3,
    near_out, t0_out, t1_out, t2_out, basis_out, above_out,
    rhs_v, pts_v, basis_v, c0_v, s0_v, near_v, sems, chunk_sems, out_sems,
):
    ahead = copies(
        [
            (t_lower, above_out.at[pl.ds(0, 4)]),
            (t_upper, above_out.at[pl.ds(4, 1)]),
        ], sems)

    def arrivals(step):
        cols = pl.ds(pl.multiple_of(step * 2048, 2048), 2048)
        return copies(
            [
                (pts.at[:, cols], pts_v.at[step]), (rhs.at[:, cols], rhs_v.at[step]),
                (c0.at[step], c0_v.at[step]), (s0.at[step], s0_v.at[step]),
                (basis.at[pl.ds(step * 4, 4)], basis_v.at[step]),
            ], chunk_sems, 5 * step)

    def departure(step):
        return pltpu.make_async_copy(near_v.at[step], near_out.at[step], out_sems.at[step])

    for step in range(4):
        for copy in arrivals(step):
            copy.start()
    for copy in ahead:
        copy.start()

    def chunk(step, carry):
        for copy in arrivals(step):
            copy.wait()
        for q in range(4):
            leaf = slice(512 * q, 512 * (q + 1))
            x = rhs_v[step, :, leaf]
            left, right = operands(*halves(pts_v[step, :, leaf] * SCALE))
            wide = jnp.exp2(mm_tn(left[:, :256], right)).astype(BF)
            last = jnp.exp2(mm_tn(left[:, 256:], right[:, 256:])).astype(BF)
            both = mm(x[:, :256], wide) + RIDGE * x.astype(F32)
            first = both[:, :256] + mm_nt(x[:, 256:], wide[:, 256:])
            second = both[:, 256:] + mm(x[:, 256:], last)
            near_v[step, :, leaf] = jnp.concatenate([first, second], axis=1).astype(BF)
        departure(step).start()
        for q in range(4):
            basis_out[4 * step + q] = basis_v[step, q].T
        t0_out[step] = sibling_sum(c0_v[step], *operands(s0_v[step, :32, :], s0_v[step, 32:, :]))
        return carry

    lax.fori_loop(0, 4, chunk, 0)
    t1_out[...] = sibling_sum(c1[...], *operands(s1[:32, :], s1[32:, :]))
    mine = lax.axis_index("leaf") % 4
    target, _ = operands(got[mine, 96:128, :], got[mine, 128:160, :])

    def side(rows):
        return jnp.concatenate([got[k, rows, :] for k in range(4)], axis=1)

    _, source = operands(side(slice(96, 128)), side(slice(128, 160)))
    hi, lo = halves(jnp.exp2(mm_tn(target, source)))
    c2 = jnp.concatenate(
        [jnp.where(mine == k, 0.0, got[k, 0:32, :].astype(F32)) for k in range(4)], axis=1
    ).astype(BF)
    t2_out[...] = mm_nt(c2, hi) + mm_nt(c2, lo)
    for copy in ahead:
        copy.wait()
    for step in range(4):
        departure(step).wait()


def top_kernel(got, place3, near, t_leaf, out, near_out, tl_out, sems):
    ahead = copies([(t_leaf, tl_out), (near, near_out)], sems)
    for copy in ahead:
        copy.start()
    node = lax.axis_index("leaf") // 4
    target, _ = operands(place3[:32, :], place3[32:, :])
    low = lax.broadcasted_iota(jnp.int32, (48, 128), 1) < 64
    column = lax.broadcasted_iota(jnp.int32, (32, 512), 1)
    acc = jnp.zeros((32, 128), F32)
    for first in range(0, 32, 8):
        parts = []
        for k in range(first, first + 8, 2):
            even, odd = got[k].astype(F32), got[k + 1].astype(F32)
            parts.append(jnp.concatenate([
                jnp.where(low, even, pltpu.roll(odd, 64, 1)),
                jnp.where(low, pltpu.roll(even, 64, 1), odd),
            ], axis=0))
        rows = jnp.concatenate(parts, axis=1)
        c3 = jnp.where(column // 64 == node - first, 0.0, rows[:32]).astype(BF)
        _, source = operands(rows[32:64].astype(BF), rows[64:].astype(BF))
        hi, lo = halves(jnp.exp2(mm_tn(target, source)))
        acc = acc + mm_nt(c3, hi) + mm_nt(c3, lo)
    out[...] = acc
    for copy in ahead:
        copy.wait()


def down_kernel(
    part, other, t0, t1, t2, near, basis, t_leaf, above,
    out, out_v, out_sems,
):
    def departure(step):
        cols = pl.ds(pl.multiple_of(step * 2048, 2048), 2048)
        return pltpu.make_async_copy(out_v.at[step], out.at[:, cols], out_sems.at[step])

    t3 = part[...] + other[...]
    g2 = t2[...] + fold(mm_nt(stacked(t3), above[4]))
    g1 = t1[...] + fold(mm_nt(stacked(g2), above[:4].reshape(512, 128)))
    g0 = []
    for step in range(4):
        here = stacked(g1[:, 128 * step:128 * (step + 1)])
        g0.append((t0[step] + fold(mm_nt(here, t_leaf[4 * step:4 * step + 4].reshape(512, 128)))).astype(BF))
    for step in range(4):
        for q in range(4):
            cols = slice(512 * q, 512 * (q + 1))
            far = mm(g0[step][:, 128 * q:128 * (q + 1)], basis[4 * step + q])
            out_v[step, :, cols] = (near[step, :, cols].astype(F32) + far).astype(BF)
        departure(step).start()
    for step in range(4):
        departure(step).wait()


def call(kernel, name, ins, outs, scratch=(), cost=None, **kwargs):
    spec = lambda space: pl.BlockSpec(memory_space=space)
    return pl.pallas_call(
        kernel,
        in_specs=[spec(space) for _, space in ins],
        out_specs=[spec(space) for _, _, space in outs],
        out_shape=[
            (space if space is not pl.ANY else jax.ShapeDtypeStruct)(shape, dtype)
            for shape, dtype, space in outs
        ],
        scratch_shapes=list(scratch),
        compiler_params=pltpu.CompilerParams(vmem_limit_bytes=VMEM_LIMIT),
        cost_estimate=cost,
        name=name,
    )(*[pltpu.with_memory_space_constraint(x, space) for x, space in ins])


def per_device(
    rhs_block, points, basis, skeleton_leaf, skeleton_lower, skeleton_upper,
    skeleton_top, transfer_leaf, transfer_lower, transfer_upper,
):
    vmem, hbm, dma = pltpu.VMEM, pltpu.HBM, pltpu.SemaphoreType.DMA
    i32 = jnp.int32

    def inside(*arrays):
        return [(x, vmem) for x in arrays]

    def outside(*arrays):
        return [(x, hbm) for x in arrays]

    transfers = (transfer_leaf, transfer_lower, transfer_upper)
    top_index, c0, s0, c1, s1, msg1 = call(
        up_kernel, "upward",
        outside(
            rhs_block, points, basis, skeleton_leaf, skeleton_lower, skeleton_upper,
            skeleton_top, *transfers),
        [
            ((32, 128), i32, vmem), ((4, 32, 512), F32, hbm), ((4, 64, 512), BF, hbm),
            ((32, 512), F32, vmem), ((64, 512), BF, vmem), ((4, 160, 128), BF, vmem),
        ],
        [
            vmem((4, 32, 2048), BF), vmem((4, 32, 2048), F32), vmem((4, 4, 512, 128), BF),
            vmem((4, 4, 128, 128), BF), vmem((4, 128, 128), BF), vmem((1, 128, 128), BF),
            vmem((16, 128), i32), vmem((4, 128), i32), vmem((1, 128), i32),
            vmem((4, 32, 512), F32), vmem((4, 64, 512), BF), dma((6,)), dma((16,)), dma((8,)),
        ],
        pl.CostEstimate(flops=10**9, bytes_accessed=5 * 10**6, transcendentals=0),
    )

    nodes = lax.axis_size("leaf") // 4
    siblings = [[4 * k + i for i in range(4)] for k in range(nodes)]
    turn = (0, 0, 1, 1)
    across = [
        [4 * k + 2 * (turn[k % 4] ^ chip) + core for k in range(nodes)]
        for chip in range(2) for core in range(2)
    ]
    got1 = lax.all_to_all(msg1, "leaf", 0, 0, axis_index_groups=siblings, tiled=True)

    msg2, place3 = call(
        mid_kernel, "middle", inside(got1, top_index),
        [((32, 48, 128), BF, vmem), ((64, 128), BF, vmem)],
    )

    got2 = lax.all_to_all(msg2, "leaf", 0, 0, axis_index_groups=across, tiled=True)

    near, t0, t1, t2, gens, above = call(
        near_kernel, "near",
        outside(rhs_block, points, basis, transfer_lower, transfer_upper, c0, s0)
        + inside(c1, s1, got1, place3),
        [
            ((4, 32, 2048), BF, hbm), ((4, 32, 512), F32, vmem),
            ((32, 512), F32, vmem), ((32, 128), F32, vmem),
            ((16, 128, 512), BF, vmem), ((5, 128, 128), BF, vmem),
        ],
        [
            vmem((4, 32, 2048), BF), vmem((4, 32, 2048), F32), vmem((4, 4, 512, 128), BF),
            vmem((4, 32, 512), F32), vmem((4, 64, 512), BF), vmem((4, 32, 2048), BF),
            dma((2,)), dma((20,)), dma((4,)),
        ],
        pl.CostEstimate(flops=6 * 10**9, bytes_accessed=3 * 10**6, transcendentals=5 * 10**6),
    )

    part, near, t_leaf = call(
        top_kernel, "top", inside(got2, place3) + outside(near, transfer_leaf),
        [((32, 128), F32, vmem), ((4, 32, 2048), BF, vmem), ((16, 128, 128), BF, vmem)],
        [dma((2,))],
    )

    partner = [(i, i ^ 1) for i in range(4 * nodes)]
    other = lax.ppermute(part, "leaf", partner)

    product, = call(
        down_kernel, "downward",
        inside(part, other, t0, t1, t2, near, gens, t_leaf, above),
        [((32, 8192), BF, hbm)],
        [
            vmem((4, 32, 2048), BF), dma((4,)),
        ],
        pl.CostEstimate(flops=2 * 10**9, bytes_accessed=5 * 10**6, transcendentals=10**6),
    )
    return product


def solution(mesh):
    return jax.shard_map(
        per_device,
        mesh=mesh,
        in_specs=(
            P("rhs", "leaf"),
            P(None, "leaf"),
            P("leaf", None, None),
            P("leaf", None),
            P("leaf", None),
            P("leaf", None),
            P(),
            P("leaf", None, None),
            P("leaf", None, None),
            P("leaf", None, None),
        ),
        out_specs=P("rhs", "leaf"),
        check_vma=False,
    )
```

```python
import jax
import jax.numpy as jnp
from jax import lax
from jax.experimental import pallas as pl
from jax.experimental.pallas import tpu as pltpu
from jax.sharding import PartitionSpec as P

RIDGE = 1.0
SCALE = (2.0 * 1.4426950408889634) ** 0.5
BF = jnp.bfloat16
PLACE_STEPS = 12800.0
LOG_STEPS = 128.0
LOG_ZERO = 127.0
F32 = jnp.float32
VMEM_LIMIT = 32 * 1024 * 1024


def mm(a, b):
    return jnp.dot(a, b, preferred_element_type=F32)


def mm_nt(a, b):
    return lax.dot_general(a, b, (((1,), (1,)), ((), ())), preferred_element_type=F32)


def mm_tn(a, b):
    return lax.dot_general(a, b, (((0,), (0,)), ((), ())), preferred_element_type=F32)


def halves(x):
    hi = x.astype(BF)
    return hi, (x - hi.astype(F32)).astype(BF)


def stacked(x):
    return jnp.concatenate(halves(x), axis=0)


def fold(x):
    rows = x.shape[0] // 2
    return x[:rows] + x[rows:]


def chosen(index, count):
    rows = lax.broadcasted_iota(jnp.int32, (count, index.shape[1]), 0)
    return jnp.where(rows == index, 1.0, 0.0).astype(BF)


def operands(h, m):
    full = h.astype(F32) + m.astype(F32)
    norm = -0.5 * jnp.sum(full * full, axis=0, keepdims=True)
    n1 = norm.astype(BF).astype(F32)
    n2 = (norm - n1).astype(BF).astype(F32)
    n3 = norm - n1 - n2
    row = lax.broadcasted_iota(jnp.int32, (16, h.shape[1]), 0)
    one = jnp.where((row >= 3) & (row < 6), 1.0, 0.0)
    left = jnp.where(row == 0, n1, jnp.where(row == 1, n2, jnp.where(row == 2, n3, one)))
    one = jnp.where(row < 3, 1.0, 0.0)
    right = jnp.where(row == 3, n1, jnp.where(row == 4, n2, jnp.where(row == 5, n3, one)))
    return (
        jnp.concatenate([h, h, m, left.astype(BF)], axis=0),
        jnp.concatenate([h, m, h, right.astype(BF)], axis=0),
    )


def copies(pairs, sems, start=0):
    return [
        pltpu.make_async_copy(src, dst, sems.at[start + k])
        for k, (src, dst) in enumerate(pairs)
    ]


def up_kernel(
    rhs, pts, basis, idx_leaf, idx_lower, idx_upper, idx_top, t_leaf, t_lower, t_upper,
    it_v, c0_out, s0_out, c1_v, s1_v, msg_v,
    rhs_v, pts_v, basis_v, tl_v, tlo_v, tu_v, il_v, ilo_v, iu_v,
    c0_v, s0_v, sems, chunk_sems, out_sems,
):
    small = copies(
        [
            (idx_leaf, il_v), (idx_lower, ilo_v), (idx_upper, iu_v), (t_lower, tlo_v),
            (t_upper, tu_v), (idx_top, it_v),
        ], sems)

    def arrivals(step):
        cols = pl.ds(pl.multiple_of(step * 2048, 2048), 2048)
        leaves = pl.ds(step * 4, 4)
        return copies(
            [
                (pts.at[:, cols], pts_v.at[step]), (rhs.at[:, cols], rhs_v.at[step]),
                (basis.at[leaves], basis_v.at[step]), (t_leaf.at[leaves], tl_v.at[step]),
            ], chunk_sems, 4 * step)

    def departures(step):
        return copies(
            [(c0_v.at[step], c0_out.at[step]), (s0_v.at[step], s0_out.at[step])],
            out_sems, 2 * step)

    small[0].start()
    for step in range(4):
        for copy in arrivals(step):
            copy.start()
        if step == 0:
            for copy in small[1:]:
                copy.start()
    small[0].wait()
    small[1].wait()

    def chunk(step, carry):
        for copy in arrivals(step):
            copy.wait()
        coeffs, places = [], []
        for q in range(4):
            cols = slice(512 * q, 512 * (q + 1))
            coeffs.append(mm(rhs_v[step, :, cols], basis_v[step, q]))
            hm = stacked(pts_v[step, :, cols] * SCALE)
            pick = chosen(il_v[pl.ds(4 * step + q, 1), :], 512)
            places.append(mm(hm, pick).astype(BF))
        c0 = jnp.concatenate(coeffs, axis=1)
        s0 = jnp.concatenate(places, axis=1)
        c0_v[step] = c0
        s0_v[step] = s0
        for copy in departures(step):
            copy.start()
        return carry

    lax.fori_loop(0, 4, chunk, 0)
    for n in range(4):
        lanes = slice(128 * n, 128 * (n + 1))
        c1_v[:, lanes] = fold(mm(stacked(c0_v[n]), tl_v[n].reshape(512, 128)))
        s1_v[:, lanes] = mm(s0_v[n], chosen(ilo_v[n:n + 1, :], 512)).astype(BF)
    for copy in small[2:]:
        copy.wait()
    c2 = fold(mm(stacked(c1_v[...]), tlo_v[...].reshape(512, 128)))
    s2 = mm(s1_v[...], chosen(iu_v[...], 512)).astype(BF)
    raised = fold(mm(stacked(c2), tu_v[0]))
    msg = jnp.concatenate([c2.astype(BF), stacked(raised), s2], axis=0)
    for k in range(4):
        msg_v[k] = msg
    for step in range(4):
        for copy in departures(step):
            copy.wait()


def mid_kernel(got, idx_top, msg_out, place_out):
    position = lax.axis_index("leaf")
    c3 = jnp.zeros((32, 128), F32)
    for k in range(4):
        c3 = c3 + got[k, 32:64, :].astype(F32) + got[k, 64:96, :].astype(F32)
    s2 = jnp.concatenate([got[k, 96:160, :] for k in range(4)], axis=1)
    s3 = mm(s2, chosen(idx_top[pl.ds(position // 4, 1), :], 512))
    place_out[...] = s3.astype(BF)
    place = jnp.floor((s3[:32] + s3[32:]) * PLACE_STEPS + 0.5)
    level = LOG_STEPS * (jnp.log2(jnp.maximum(jnp.abs(c3), 1e-38)) + LOG_ZERO)
    level = jnp.clip(jnp.floor(level + 0.5), 0.0, 32767.0)
    coeff = jnp.where(c3 < 0.0, -level, level)
    low = lax.broadcasted_iota(jnp.int32, (32, 128), 1) < 64
    first = position % 2 == 0
    msg = jnp.where(
        low,
        jnp.where(first, coeff, pltpu.roll(coeff, 64, 1)),
        jnp.where(first, pltpu.roll(place, 64, 1), place),
    ).astype(jnp.int32).astype(jnp.int16)
    for k in range(32):
        msg_out[k] = msg


def sibling_sum(c, left, right):
    chl = stacked(c)
    block = jnp.exp2(mm_tn(left, right))
    zero = jnp.zeros((128, 128), F32)
    rows = []
    for s in range(4):
        src = slice(128 * s, 128 * (s + 1))
        rows.append(jnp.concatenate(
            [zero if s == t else block[src, 128 * t:128 * (t + 1)] for t in range(4)], axis=1))
    hi, lo = halves(jnp.concatenate(rows, axis=0))
    return fold(mm(chl, hi)) + mm(chl[:32], lo)


def near_kernel(
    rhs, pts, basis, t_lower, t_upper, c0, s0, c1, s1, got, place3,
    near_out, t0_out, t1_out, t2_out, basis_out, above_out,
    rhs_v, pts_v, basis_v, c0_v, s0_v, near_v, sems, chunk_sems, out_sems,
):
    ahead = copies(
        [
            (t_lower, above_out.at[pl.ds(0, 4)]),
            (t_upper, above_out.at[pl.ds(4, 1)]),
        ], sems)

    def arrivals(step):
        cols = pl.ds(pl.multiple_of(step * 2048, 2048), 2048)
        return copies(
            [
                (pts.at[:, cols], pts_v.at[step]), (rhs.at[:, cols], rhs_v.at[step]),
                (c0.at[step], c0_v.at[step]), (s0.at[step], s0_v.at[step]),
                (basis.at[pl.ds(step * 4, 4)], basis_v.at[step]),
            ], chunk_sems, 5 * step)

    def departure(step):
        return pltpu.make_async_copy(near_v.at[step], near_out.at[step], out_sems.at[step])

    for step in range(4):
        for copy in arrivals(step):
            copy.start()
    for copy in ahead:
        copy.start()

    def chunk(step, carry):
        for copy in arrivals(step):
            copy.wait()
        for q in range(4):
            leaf = slice(512 * q, 512 * (q + 1))
            x = rhs_v[step, :, leaf]
            left, right = operands(*halves(pts_v[step, :, leaf] * SCALE))
            wide = jnp.exp2(mm_tn(left[:, :256], right)).astype(BF)
            last = jnp.exp2(mm_tn(left[:, 256:], right[:, 256:])).astype(BF)
            both = mm(x[:, :256], wide) + RIDGE * x.astype(F32)
            first = both[:, :256] + mm_nt(x[:, 256:], wide[:, 256:])
            second = both[:, 256:] + mm(x[:, 256:], last)
            near_v[step, :, leaf] = jnp.concatenate([first, second], axis=1).astype(BF)
        departure(step).start()
        for q in range(4):
            basis_out[4 * step + q] = basis_v[step, q].T
        t0_out[step] = sibling_sum(c0_v[step], *operands(s0_v[step, :32, :], s0_v[step, 32:, :]))
        return carry

    lax.fori_loop(0, 4, chunk, 0)
    t1_out[...] = sibling_sum(c1[...], *operands(s1[:32, :], s1[32:, :]))
    mine = lax.axis_index("leaf") % 4
    target, _ = operands(got[mine, 96:128, :], got[mine, 128:160, :])

    def side(rows):
        return jnp.concatenate([got[k, rows, :] for k in range(4)], axis=1)

    _, source = operands(side(slice(96, 128)), side(slice(128, 160)))
    hi, lo = halves(jnp.exp2(mm_tn(target, source)))
    c2 = jnp.concatenate(
        [jnp.where(mine == k, 0.0, got[k, 0:32, :].astype(F32)) for k in range(4)], axis=1
    ).astype(BF)
    t2_out[...] = mm_nt(c2, hi) + mm_nt(c2, lo)
    for copy in ahead:
        copy.wait()
    for step in range(4):
        departure(step).wait()


def top_kernel(got, place3, near, t_leaf, out, near_out, tl_out, sems):
    ahead = copies([(t_leaf, tl_out), (near, near_out)], sems)
    for copy in ahead:
        copy.start()
    node = lax.axis_index("leaf") // 4
    target, _ = operands(place3[:32, :], place3[32:, :])
    low = lax.broadcasted_iota(jnp.int32, (32, 128), 1) < 64
    column = lax.broadcasted_iota(jnp.int32, (32, 512), 1)
    acc = jnp.zeros((32, 128), F32)
    for first in range(0, 32, 8):
        coeffs, places = [], []
        for k in range(first, first + 8, 2):
            even = got[k].astype(jnp.int32).astype(F32)
            odd = got[k + 1].astype(jnp.int32).astype(F32)
            coeffs.append(jnp.where(low, even, pltpu.roll(odd, 64, 1)))
            places.append(jnp.where(low, pltpu.roll(even, 64, 1), odd))
        level = jnp.concatenate(coeffs, axis=1)
        size = jnp.exp2(jnp.abs(level) * (1.0 / LOG_STEPS) - LOG_ZERO)
        c3 = jnp.where(level < 0.0, -size, size)
        c3 = jnp.where((level == 0.0) | (column // 64 == node - first), 0.0, c3)
        place = jnp.concatenate(places, axis=1) * (1.0 / PLACE_STEPS)
        _, source = operands(*halves(place))
        hi, lo = halves(jnp.exp2(mm_tn(target, source)))
        chl = stacked(c3)
        acc = acc + fold(mm_nt(chl, hi)) + mm_nt(chl[:32], lo)
    out[...] = acc
    for copy in ahead:
        copy.wait()


def down_kernel(
    part, other, t0, t1, t2, near, basis, t_leaf, above,
    out, out_v, out_sems,
):
    def departure(step):
        cols = pl.ds(pl.multiple_of(step * 2048, 2048), 2048)
        return pltpu.make_async_copy(out_v.at[step], out.at[:, cols], out_sems.at[step])

    t3 = part[...] + other[...]
    g2 = t2[...] + fold(mm_nt(stacked(t3), above[4]))
    g1 = t1[...] + fold(mm_nt(stacked(g2), above[:4].reshape(512, 128)))
    g0 = []
    for step in range(4):
        here = stacked(g1[:, 128 * step:128 * (step + 1)])
        g0.append((t0[step] + fold(mm_nt(here, t_leaf[4 * step:4 * step + 4].reshape(512, 128)))).astype(BF))
    for step in range(4):
        for q in range(4):
            cols = slice(512 * q, 512 * (q + 1))
            far = mm(g0[step][:, 128 * q:128 * (q + 1)], basis[4 * step + q])
            out_v[step, :, cols] = (near[step, :, cols].astype(F32) + far).astype(BF)
        departure(step).start()
    for step in range(4):
        departure(step).wait()


def call(kernel, name, ins, outs, scratch=(), cost=None, **kwargs):
    spec = lambda space: pl.BlockSpec(memory_space=space)
    return pl.pallas_call(
        kernel,
        in_specs=[spec(space) for _, space in ins],
        out_specs=[spec(space) for _, _, space in outs],
        out_shape=[
            (space if space is not pl.ANY else jax.ShapeDtypeStruct)(shape, dtype)
            for shape, dtype, space in outs
        ],
        scratch_shapes=list(scratch),
        compiler_params=pltpu.CompilerParams(vmem_limit_bytes=VMEM_LIMIT),
        cost_estimate=cost,
        name=name,
    )(*[pltpu.with_memory_space_constraint(x, space) for x, space in ins])


def per_device(
    rhs_block, points, basis, skeleton_leaf, skeleton_lower, skeleton_upper,
    skeleton_top, transfer_leaf, transfer_lower, transfer_upper,
):
    vmem, hbm, dma = pltpu.VMEM, pltpu.HBM, pltpu.SemaphoreType.DMA
    i32 = jnp.int32

    def inside(*arrays):
        return [(x, vmem) for x in arrays]

    def outside(*arrays):
        return [(x, hbm) for x in arrays]

    transfers = (transfer_leaf, transfer_lower, transfer_upper)
    top_index, c0, s0, c1, s1, msg1 = call(
        up_kernel, "upward",
        outside(
            rhs_block, points, basis, skeleton_leaf, skeleton_lower, skeleton_upper,
            skeleton_top, *transfers),
        [
            ((32, 128), i32, vmem), ((4, 32, 512), F32, hbm), ((4, 64, 512), BF, hbm),
            ((32, 512), F32, vmem), ((64, 512), BF, vmem), ((4, 160, 128), BF, vmem),
        ],
        [
            vmem((4, 32, 2048), BF), vmem((4, 32, 2048), F32), vmem((4, 4, 512, 128), BF),
            vmem((4, 4, 128, 128), BF), vmem((4, 128, 128), BF), vmem((1, 128, 128), BF),
            vmem((16, 128), i32), vmem((4, 128), i32), vmem((1, 128), i32),
            vmem((4, 32, 512), F32), vmem((4, 64, 512), BF), dma((6,)), dma((16,)), dma((8,)),
        ],
        pl.CostEstimate(flops=10**9, bytes_accessed=5 * 10**6, transcendentals=0),
    )

    nodes = lax.axis_size("leaf") // 4
    siblings = [[4 * k + i for i in range(4)] for k in range(nodes)]
    turn = (0, 0, 1, 1)
    across = [
        [4 * k + 2 * (turn[k % 4] ^ chip) + core for k in range(nodes)]
        for chip in range(2) for core in range(2)
    ]
    got1 = lax.all_to_all(msg1, "leaf", 0, 0, axis_index_groups=siblings, tiled=True)

    msg2, place3 = call(
        mid_kernel, "middle", inside(got1, top_index),
        [((32, 32, 128), jnp.int16, vmem), ((64, 128), BF, vmem)],
    )

    got2 = lax.all_to_all(msg2, "leaf", 0, 0, axis_index_groups=across, tiled=True)

    near, t0, t1, t2, gens, above = call(
        near_kernel, "near",
        outside(rhs_block, points, basis, transfer_lower, transfer_upper, c0, s0)
        + inside(c1, s1, got1, place3),
        [
            ((4, 32, 2048), BF, hbm), ((4, 32, 512), F32, vmem),
            ((32, 512), F32, vmem), ((32, 128), F32, vmem),
            ((16, 128, 512), BF, vmem), ((5, 128, 128), BF, vmem),
        ],
        [
            vmem((4, 32, 2048), BF), vmem((4, 32, 2048), F32), vmem((4, 4, 512, 128), BF),
            vmem((4, 32, 512), F32), vmem((4, 64, 512), BF), vmem((4, 32, 2048), BF),
            dma((2,)), dma((20,)), dma((4,)),
        ],
        pl.CostEstimate(flops=6 * 10**9, bytes_accessed=3 * 10**6, transcendentals=5 * 10**6),
    )

    part, near, t_leaf = call(
        top_kernel, "top", inside(got2, place3) + outside(near, transfer_leaf),
        [((32, 128), F32, vmem), ((4, 32, 2048), BF, vmem), ((16, 128, 128), BF, vmem)],
        [dma((2,))],
    )

    partner = [(i, i ^ 1) for i in range(4 * nodes)]
    other = lax.ppermute(part, "leaf", partner)

    product, = call(
        down_kernel, "downward",
        inside(part, other, t0, t1, t2, near, gens, t_leaf, above),
        [((32, 8192), BF, hbm)],
        [
            vmem((4, 32, 2048), BF), dma((4,)),
        ],
        pl.CostEstimate(flops=2 * 10**9, bytes_accessed=5 * 10**6, transcendentals=10**6),
    )
    return product


def solution(mesh):
    return jax.shard_map(
        per_device,
        mesh=mesh,
        in_specs=(
            P("rhs", "leaf"),
            P(None, "leaf"),
            P("leaf", None, None),
            P("leaf", None),
            P("leaf", None),
            P("leaf", None),
            P(),
            P("leaf", None, None),
            P("leaf", None, None),
            P("leaf", None, None),
        ),
        out_specs=P("rhs", "leaf"),
        check_vma=False,
    )
```

```python
import jax
import jax.numpy as jnp
from jax import lax
from jax.experimental import pallas as pl
from jax.experimental.pallas import tpu as pltpu
from jax.sharding import PartitionSpec as P

RIDGE = 1.0
SCALE = (2.0 * 1.4426950408889634) ** 0.5
BF = jnp.bfloat16
PLACE_STEPS = 12800.0
LOG_STEPS = 128.0
LOG_ZERO = 127.0
F32 = jnp.float32
VMEM_LIMIT = 32 * 1024 * 1024


def mm(a, b):
    return jnp.dot(a, b, preferred_element_type=F32)


def mm_nt(a, b):
    return lax.dot_general(a, b, (((1,), (1,)), ((), ())), preferred_element_type=F32)


def mm_tn(a, b):
    return lax.dot_general(a, b, (((0,), (0,)), ((), ())), preferred_element_type=F32)


def halves(x):
    hi = x.astype(BF)
    return hi, (x - hi.astype(F32)).astype(BF)


def stacked(x):
    return jnp.concatenate(halves(x), axis=0)


def fold(x):
    rows = x.shape[0] // 2
    return x[:rows] + x[rows:]


def chosen(index, count):
    rows = lax.broadcasted_iota(jnp.int32, (count, index.shape[1]), 0)
    return jnp.where(rows == index, 1.0, 0.0).astype(BF)


def operands(h, m):
    full = h.astype(F32) + m.astype(F32)
    norm = -0.5 * jnp.sum(full * full, axis=0, keepdims=True)
    n1 = norm.astype(BF).astype(F32)
    n2 = (norm - n1).astype(BF).astype(F32)
    n3 = norm - n1 - n2
    row = lax.broadcasted_iota(jnp.int32, (16, h.shape[1]), 0)
    one = jnp.where((row >= 3) & (row < 6), 1.0, 0.0)
    left = jnp.where(row == 0, n1, jnp.where(row == 1, n2, jnp.where(row == 2, n3, one)))
    one = jnp.where(row < 3, 1.0, 0.0)
    right = jnp.where(row == 3, n1, jnp.where(row == 4, n2, jnp.where(row == 5, n3, one)))
    return (
        jnp.concatenate([h, h, m, left.astype(BF)], axis=0),
        jnp.concatenate([h, m, h, right.astype(BF)], axis=0),
    )


def copies(pairs, sems, start=0):
    return [
        pltpu.make_async_copy(src, dst, sems.at[start + k])
        for k, (src, dst) in enumerate(pairs)
    ]


def up_kernel(
    rhs, pts, basis, idx_leaf, idx_lower, idx_upper, idx_top, t_leaf, t_lower, t_upper,
    it_v, c0_out, s0_out, c1_v, s1_v, msg_v,
    rhs_v, pts_v, basis_v, tl_v, tlo_v, tu_v, il_v, ilo_v, iu_v,
    c0_v, s0_v, sems, chunk_sems, out_sems,
):
    small = copies(
        [
            (idx_leaf, il_v), (idx_lower, ilo_v), (idx_upper, iu_v), (t_lower, tlo_v),
            (t_upper, tu_v), (idx_top, it_v),
        ], sems)

    def arrivals(step):
        cols = pl.ds(pl.multiple_of(step * 2048, 2048), 2048)
        leaves = pl.ds(step * 4, 4)
        return copies(
            [
                (pts.at[:, cols], pts_v.at[step]), (rhs.at[:, cols], rhs_v.at[step]),
                (basis.at[leaves], basis_v.at[step]), (t_leaf.at[leaves], tl_v.at[step]),
            ], chunk_sems, 4 * step)

    def departures(step):
        return copies(
            [(c0_v.at[step], c0_out.at[step]), (s0_v.at[step], s0_out.at[step])],
            out_sems, 2 * step)

    small[0].start()
    for step in range(4):
        for copy in arrivals(step):
            copy.start()
        if step == 0:
            for copy in small[1:]:
                copy.start()
    small[0].wait()
    small[1].wait()

    def chunk(step, carry):
        for copy in arrivals(step):
            copy.wait()
        coeffs, places = [], []
        for q in range(4):
            cols = slice(512 * q, 512 * (q + 1))
            coeffs.append(mm(rhs_v[step, :, cols], basis_v[step, q]))
            hm = stacked(pts_v[step, :, cols] * SCALE)
            pick = chosen(il_v[pl.ds(4 * step + q, 1), :], 512)
            places.append(mm(hm, pick).astype(BF))
        c0 = jnp.concatenate(coeffs, axis=1)
        s0 = jnp.concatenate(places, axis=1)
        c0_v[step] = c0
        s0_v[step] = s0
        for copy in departures(step):
            copy.start()
        return carry

    lax.fori_loop(0, 4, chunk, 0)
    for n in range(4):
        lanes = slice(128 * n, 128 * (n + 1))
        c1_v[:, lanes] = fold(mm(stacked(c0_v[n]), tl_v[n].reshape(512, 128)))
        s1_v[:, lanes] = mm(s0_v[n], chosen(ilo_v[n:n + 1, :], 512)).astype(BF)
    for copy in small[2:]:
        copy.wait()
    c2 = fold(mm(stacked(c1_v[...]), tlo_v[...].reshape(512, 128)))
    s2 = mm(s1_v[...], chosen(iu_v[...], 512)).astype(BF)
    raised = fold(mm(stacked(c2), tu_v[0]))
    hi = raised.astype(BF).astype(F32)
    lo = raised - hi
    low = lax.broadcasted_iota(jnp.int32, (32, 128), 1) < 64
    halved = (
        jnp.where(low, hi, pltpu.roll(lo, 64, 1)),
        jnp.where(low, pltpu.roll(hi, 64, 1), lo),
    )
    for k in range(4):
        msg_v[k] = jnp.concatenate([c2.astype(BF), halved[k % 2].astype(BF), s2], axis=0)
    for step in range(4):
        for copy in departures(step):
            copy.wait()


def mid_kernel(got, idx_top, msg_out, place_out):
    position = lax.axis_index("leaf")
    raised = jnp.zeros((32, 128), F32)
    for k in range(4):
        raised = raised + got[k, 32:64, :].astype(F32)
    c3 = raised + pltpu.roll(raised, 64, 1)
    s2 = jnp.concatenate([got[k, 64:128, :] for k in range(4)], axis=1)
    s3 = mm(s2, chosen(idx_top[pl.ds(position // 4, 1), :], 512))
    place_out[...] = s3.astype(BF)
    place = jnp.floor((s3[:32] + s3[32:]) * PLACE_STEPS + 0.5)
    level = LOG_STEPS * (jnp.log2(jnp.maximum(jnp.abs(c3), 1e-38)) + LOG_ZERO)
    level = jnp.clip(jnp.floor(level + 0.5), 0.0, 32767.0)
    coeff = jnp.where(c3 < 0.0, -level, level)
    low = lax.broadcasted_iota(jnp.int32, (32, 128), 1) < 64
    first = position % 2 == 0
    msg = jnp.where(
        low, coeff, jnp.where(first, pltpu.roll(place, 64, 1), place)
    ).astype(jnp.int32).astype(jnp.int16)
    for k in range(32):
        msg_out[k] = msg


def sibling_sum(c, left, right):
    chl = stacked(c)
    block = jnp.exp2(mm_tn(left, right))
    zero = jnp.zeros((128, 128), F32)
    rows = []
    for s in range(4):
        src = slice(128 * s, 128 * (s + 1))
        rows.append(jnp.concatenate(
            [zero if s == t else block[src, 128 * t:128 * (t + 1)] for t in range(4)], axis=1))
    hi, lo = halves(jnp.concatenate(rows, axis=0))
    return fold(mm(chl, hi)) + mm(chl[:32], lo)


def near_kernel(
    rhs, pts, basis, t_lower, t_upper, c0, s0, c1, s1, got, place3,
    near_out, t0_out, t1_out, t2_out, basis_out, above_out,
    rhs_v, pts_v, basis_v, c0_v, s0_v, near_v, sems, chunk_sems, out_sems,
):
    ahead = copies(
        [
            (t_lower, above_out.at[pl.ds(0, 4)]),
            (t_upper, above_out.at[pl.ds(4, 1)]),
        ], sems)

    def arrivals(step):
        cols = pl.ds(pl.multiple_of(step * 2048, 2048), 2048)
        return copies(
            [
                (pts.at[:, cols], pts_v.at[step]), (rhs.at[:, cols], rhs_v.at[step]),
                (c0.at[step], c0_v.at[step]), (s0.at[step], s0_v.at[step]),
                (basis.at[pl.ds(step * 4, 4)], basis_v.at[step]),
            ], chunk_sems, 5 * step)

    def departure(step):
        return pltpu.make_async_copy(near_v.at[step], near_out.at[step], out_sems.at[step])

    for step in range(4):
        for copy in arrivals(step):
            copy.start()
    for copy in ahead:
        copy.start()

    def chunk(step, carry):
        for copy in arrivals(step):
            copy.wait()
        for q in range(4):
            leaf = slice(512 * q, 512 * (q + 1))
            x = rhs_v[step, :, leaf]
            left, right = operands(*halves(pts_v[step, :, leaf] * SCALE))
            wide = jnp.exp2(mm_tn(left[:, :256], right)).astype(BF)
            last = jnp.exp2(mm_tn(left[:, 256:], right[:, 256:])).astype(BF)
            both = mm(x[:, :256], wide) + RIDGE * x.astype(F32)
            first = both[:, :256] + mm_nt(x[:, 256:], wide[:, 256:])
            second = both[:, 256:] + mm(x[:, 256:], last)
            near_v[step, :, leaf] = jnp.concatenate([first, second], axis=1).astype(BF)
        departure(step).start()
        for q in range(4):
            basis_out[4 * step + q] = basis_v[step, q].T
        t0_out[step] = sibling_sum(c0_v[step], *operands(s0_v[step, :32, :], s0_v[step, 32:, :]))
        return carry

    lax.fori_loop(0, 4, chunk, 0)
    t1_out[...] = sibling_sum(c1[...], *operands(s1[:32, :], s1[32:, :]))
    mine = lax.axis_index("leaf") % 4
    target, _ = operands(got[mine, 64:96, :], got[mine, 96:128, :])

    def side(rows):
        return jnp.concatenate([got[k, rows, :] for k in range(4)], axis=1)

    _, source = operands(side(slice(64, 96)), side(slice(96, 128)))
    hi, lo = halves(jnp.exp2(mm_tn(target, source)))
    c2 = jnp.concatenate(
        [jnp.where(mine == k, 0.0, got[k, 0:32, :].astype(F32)) for k in range(4)], axis=1
    ).astype(BF)
    t2_out[...] = mm_nt(c2, hi) + mm_nt(c2, lo)
    for copy in ahead:
        copy.wait()
    for step in range(4):
        departure(step).wait()


def top_kernel(got, place3, near, t_leaf, out, near_out, tl_out, sems):
    ahead = copies([(t_leaf, tl_out), (near, near_out)], sems)
    for copy in ahead:
        copy.start()
    node = lax.axis_index("leaf") // 4
    target, _ = operands(place3[:32, :], place3[32:, :])
    low = lax.broadcasted_iota(jnp.int32, (32, 128), 1) < 64
    column = lax.broadcasted_iota(jnp.int32, (32, 512), 1)
    acc = jnp.zeros((32, 128), F32)
    for first in range(0, 32, 8):
        coeffs, places = [], []
        for k in range(first, first + 8, 2):
            even = got[k].astype(jnp.int32).astype(F32)
            odd = got[k + 1].astype(jnp.int32).astype(F32)
            coeffs.append(jnp.where(low, even, pltpu.roll(odd, 64, 1)))
            places.append(jnp.where(low, pltpu.roll(even, 64, 1), odd))
        level = jnp.concatenate(coeffs, axis=1)
        size = jnp.exp2(jnp.abs(level) * (1.0 / LOG_STEPS) - LOG_ZERO)
        c3 = jnp.where(level < 0.0, -size, size)
        c3 = jnp.where((level == 0.0) | (column // 64 == node - first), 0.0, c3)
        place = jnp.concatenate(places, axis=1) * (1.0 / PLACE_STEPS)
        _, source = operands(*halves(place))
        hi, lo = halves(jnp.exp2(mm_tn(target, source)))
        chl = stacked(c3)
        acc = acc + fold(mm_nt(chl, hi)) + mm_nt(chl[:32], lo)
    out[...] = acc
    for copy in ahead:
        copy.wait()


def down_kernel(
    part, other, t0, t1, t2, near, basis, t_leaf, above,
    out, out_v, out_sems,
):
    def departure(step):
        cols = pl.ds(pl.multiple_of(step * 2048, 2048), 2048)
        return pltpu.make_async_copy(out_v.at[step], out.at[:, cols], out_sems.at[step])

    t3 = part[...] + other[...]
    g2 = t2[...] + fold(mm_nt(stacked(t3), above[4]))
    g1 = t1[...] + fold(mm_nt(stacked(g2), above[:4].reshape(512, 128)))
    g0 = []
    for step in range(4):
        here = stacked(g1[:, 128 * step:128 * (step + 1)])
        g0.append((t0[step] + fold(mm_nt(here, t_leaf[4 * step:4 * step + 4].reshape(512, 128)))).astype(BF))
    for step in range(4):
        for q in range(4):
            cols = slice(512 * q, 512 * (q + 1))
            far = mm(g0[step][:, 128 * q:128 * (q + 1)], basis[4 * step + q])
            out_v[step, :, cols] = (near[step, :, cols].astype(F32) + far).astype(BF)
        departure(step).start()
    for step in range(4):
        departure(step).wait()


def call(kernel, name, ins, outs, scratch=(), cost=None, **kwargs):
    spec = lambda space: pl.BlockSpec(memory_space=space)
    return pl.pallas_call(
        kernel,
        in_specs=[spec(space) for _, space in ins],
        out_specs=[spec(space) for _, _, space in outs],
        out_shape=[
            (space if space is not pl.ANY else jax.ShapeDtypeStruct)(shape, dtype)
            for shape, dtype, space in outs
        ],
        scratch_shapes=list(scratch),
        compiler_params=pltpu.CompilerParams(vmem_limit_bytes=VMEM_LIMIT),
        cost_estimate=cost,
        name=name,
    )(*[pltpu.with_memory_space_constraint(x, space) for x, space in ins])


def per_device(
    rhs_block, points, basis, skeleton_leaf, skeleton_lower, skeleton_upper,
    skeleton_top, transfer_leaf, transfer_lower, transfer_upper,
):
    vmem, hbm, dma = pltpu.VMEM, pltpu.HBM, pltpu.SemaphoreType.DMA
    i32 = jnp.int32

    def inside(*arrays):
        return [(x, vmem) for x in arrays]

    def outside(*arrays):
        return [(x, hbm) for x in arrays]

    transfers = (transfer_leaf, transfer_lower, transfer_upper)
    top_index, c0, s0, c1, s1, msg1 = call(
        up_kernel, "upward",
        outside(
            rhs_block, points, basis, skeleton_leaf, skeleton_lower, skeleton_upper,
            skeleton_top, *transfers),
        [
            ((32, 128), i32, vmem), ((4, 32, 512), F32, hbm), ((4, 64, 512), BF, hbm),
            ((32, 512), F32, vmem), ((64, 512), BF, vmem), ((4, 128, 128), BF, vmem),
        ],
        [
            vmem((4, 32, 2048), BF), vmem((4, 32, 2048), F32), vmem((4, 4, 512, 128), BF),
            vmem((4, 4, 128, 128), BF), vmem((4, 128, 128), BF), vmem((1, 128, 128), BF),
            vmem((16, 128), i32), vmem((4, 128), i32), vmem((1, 128), i32),
            vmem((4, 32, 512), F32), vmem((4, 64, 512), BF), dma((6,)), dma((16,)), dma((8,)),
        ],
        pl.CostEstimate(flops=10**9, bytes_accessed=5 * 10**6, transcendentals=0),
    )

    nodes = lax.axis_size("leaf") // 4
    siblings = [[4 * k + i for i in range(4)] for k in range(nodes)]
    turn = (0, 0, 1, 1)
    across = [
        [4 * k + 2 * (turn[k % 4] ^ chip) + core for k in range(nodes)]
        for chip in range(2) for core in range(2)
    ]
    got1 = lax.all_to_all(msg1, "leaf", 0, 0, axis_index_groups=siblings, tiled=True)

    msg2, place3 = call(
        mid_kernel, "middle", inside(got1, top_index),
        [((32, 32, 128), jnp.int16, vmem), ((64, 128), BF, vmem)],
    )

    got2 = lax.all_to_all(msg2, "leaf", 0, 0, axis_index_groups=across, tiled=True)

    near, t0, t1, t2, gens, above = call(
        near_kernel, "near",
        outside(rhs_block, points, basis, transfer_lower, transfer_upper, c0, s0)
        + inside(c1, s1, got1, place3),
        [
            ((4, 32, 2048), BF, hbm), ((4, 32, 512), F32, vmem),
            ((32, 512), F32, vmem), ((32, 128), F32, vmem),
            ((16, 128, 512), BF, vmem), ((5, 128, 128), BF, vmem),
        ],
        [
            vmem((4, 32, 2048), BF), vmem((4, 32, 2048), F32), vmem((4, 4, 512, 128), BF),
            vmem((4, 32, 512), F32), vmem((4, 64, 512), BF), vmem((4, 32, 2048), BF),
            dma((2,)), dma((20,)), dma((4,)),
        ],
        pl.CostEstimate(flops=6 * 10**9, bytes_accessed=3 * 10**6, transcendentals=5 * 10**6),
    )

    part, near, t_leaf = call(
        top_kernel, "top", inside(got2, place3) + outside(near, transfer_leaf),
        [((32, 128), F32, vmem), ((4, 32, 2048), BF, vmem), ((16, 128, 128), BF, vmem)],
        [dma((2,))],
    )

    partner = [(i, i ^ 1) for i in range(4 * nodes)]
    other = lax.ppermute(part, "leaf", partner)

    product, = call(
        down_kernel, "downward",
        inside(part, other, t0, t1, t2, near, gens, t_leaf, above),
        [((32, 8192), BF, hbm)],
        [
            vmem((4, 32, 2048), BF), dma((4,)),
        ],
        pl.CostEstimate(flops=2 * 10**9, bytes_accessed=5 * 10**6, transcendentals=10**6),
    )
    return product


def solution(mesh):
    return jax.shard_map(
        per_device,
        mesh=mesh,
        in_specs=(
            P("rhs", "leaf"),
            P(None, "leaf"),
            P("leaf", None, None),
            P("leaf", None),
            P("leaf", None),
            P("leaf", None),
            P(),
            P("leaf", None, None),
            P("leaf", None, None),
            P("leaf", None, None),
        ),
        out_specs=P("rhs", "leaf"),
        check_vma=False,
    )
```

```python
import jax
import jax.numpy as jnp
from jax import lax
from jax.experimental import pallas as pl
from jax.experimental.pallas import tpu as pltpu
from jax.sharding import PartitionSpec as P

RIDGE = 1.0
SCALE = (2.0 * 1.4426950408889634) ** 0.5
BF = jnp.bfloat16
PLACE_STEPS = 12800.0
LOG_STEPS = 128.0
LOG_ZERO = 127.0
F32 = jnp.float32
VMEM_LIMIT = 32 * 1024 * 1024


def mm(a, b):
    return jnp.dot(a, b, preferred_element_type=F32)


def mm_nt(a, b):
    return lax.dot_general(a, b, (((1,), (1,)), ((), ())), preferred_element_type=F32)


def mm_tn(a, b):
    return lax.dot_general(a, b, (((0,), (0,)), ((), ())), preferred_element_type=F32)


def halves(x):
    hi = x.astype(BF)
    return hi, (x - hi.astype(F32)).astype(BF)


def stacked(x):
    return jnp.concatenate(halves(x), axis=0)


def fold(x):
    rows = x.shape[0] // 2
    return x[:rows] + x[rows:]


def chosen(index, count):
    rows = lax.broadcasted_iota(jnp.int32, (count, index.shape[1]), 0)
    return jnp.where(rows == index, 1.0, 0.0).astype(BF)


def operands(h, m):
    full = h.astype(F32) + m.astype(F32)
    norm = -0.5 * jnp.sum(full * full, axis=0, keepdims=True)
    n1 = norm.astype(BF).astype(F32)
    n2 = (norm - n1).astype(BF).astype(F32)
    n3 = norm - n1 - n2
    row = lax.broadcasted_iota(jnp.int32, (16, h.shape[1]), 0)
    one = jnp.where((row >= 3) & (row < 6), 1.0, 0.0)
    left = jnp.where(row == 0, n1, jnp.where(row == 1, n2, jnp.where(row == 2, n3, one)))
    one = jnp.where(row < 3, 1.0, 0.0)
    right = jnp.where(row == 3, n1, jnp.where(row == 4, n2, jnp.where(row == 5, n3, one)))
    return (
        jnp.concatenate([h, h, m, left.astype(BF)], axis=0),
        jnp.concatenate([h, m, h, right.astype(BF)], axis=0),
    )


def copies(pairs, sems, start=0):
    return [
        pltpu.make_async_copy(src, dst, sems.at[start + k])
        for k, (src, dst) in enumerate(pairs)
    ]


def up_kernel(
    rhs, pts, basis, idx_leaf, idx_lower, idx_upper, idx_top, t_leaf, t_lower, t_upper,
    it_v, c0_out, s0_out, c1_v, s1_v, msg_v,
    rhs_v, pts_v, basis_v, tl_v, tlo_v, tu_v, il_v, ilo_v, iu_v,
    c0_v, s0_v, sems, chunk_sems, out_sems,
):
    small = copies(
        [
            (idx_leaf, il_v), (idx_lower, ilo_v), (idx_upper, iu_v), (t_lower, tlo_v),
            (t_upper, tu_v), (idx_top, it_v),
        ], sems)

    def arrivals(step):
        cols = pl.ds(pl.multiple_of(step * 2048, 2048), 2048)
        leaves = pl.ds(step * 4, 4)
        return copies(
            [
                (pts.at[:, cols], pts_v.at[step]), (rhs.at[:, cols], rhs_v.at[step]),
                (basis.at[leaves], basis_v.at[step]), (t_leaf.at[leaves], tl_v.at[step]),
            ], chunk_sems, 4 * step)

    def departures(step):
        return copies(
            [(c0_v.at[step], c0_out.at[step]), (s0_v.at[step], s0_out.at[step])],
            out_sems, 2 * step)

    small[0].start()
    for step in range(4):
        for copy in arrivals(step):
            copy.start()
        if step == 0:
            for copy in small[1:]:
                copy.start()
    small[0].wait()
    small[1].wait()

    def chunk(step, carry):
        for copy in arrivals(step):
            copy.wait()
        coeffs, places = [], []
        for q in range(4):
            cols = slice(512 * q, 512 * (q + 1))
            coeffs.append(mm(rhs_v[step, :, cols], basis_v[step, q]))
            hm = stacked(pts_v[step, :, cols] * SCALE)
            pick = chosen(il_v[pl.ds(4 * step + q, 1), :], 512)
            places.append(mm(hm, pick).astype(BF))
        c0 = jnp.concatenate(coeffs, axis=1)
        s0 = jnp.concatenate(places, axis=1)
        c0_v[step] = c0
        s0_v[step] = s0
        for copy in departures(step):
            copy.start()
        return carry

    lax.fori_loop(0, 4, chunk, 0)
    for n in range(4):
        lanes = slice(128 * n, 128 * (n + 1))
        c1_v[:, lanes] = fold(mm(stacked(c0_v[n]), tl_v[n].reshape(512, 128)))
        s1_v[:, lanes] = mm(s0_v[n], chosen(ilo_v[n:n + 1, :], 512)).astype(BF)
    for copy in small[2:]:
        copy.wait()
    c2 = fold(mm(stacked(c1_v[...]), tlo_v[...].reshape(512, 128)))
    s2 = mm(s1_v[...], chosen(iu_v[...], 512)).astype(BF)
    raised = fold(mm(stacked(c2), tu_v[0]))
    hi = raised.astype(BF).astype(F32)
    lo = raised - hi
    low = lax.broadcasted_iota(jnp.int32, (32, 128), 1) < 64
    halved = (
        jnp.where(low, hi, pltpu.roll(lo, 64, 1)),
        jnp.where(low, pltpu.roll(hi, 64, 1), lo),
    )
    for k in range(4):
        msg_v[k] = jnp.concatenate([c2.astype(BF), halved[k % 2].astype(BF), s2], axis=0)
    for step in range(4):
        for copy in departures(step):
            copy.wait()


def mid_kernel(got, idx_top, msg_out, place_out):
    position = lax.axis_index("leaf")
    raised = jnp.zeros((32, 128), F32)
    for k in range(4):
        raised = raised + got[k, 32:64, :].astype(F32)
    c3 = raised + pltpu.roll(raised, 64, 1)
    s2 = jnp.concatenate([got[k, 64:128, :] for k in range(4)], axis=1)
    s3 = mm(s2, chosen(idx_top[pl.ds(position // 4, 1), :], 512))
    place_out[...] = s3.astype(BF)
    place = jnp.floor((s3[:32] + s3[32:]) * PLACE_STEPS + 0.5)
    level = LOG_STEPS * (jnp.log2(jnp.maximum(jnp.abs(c3), 1e-38)) + LOG_ZERO)
    level = jnp.clip(jnp.floor(level + 0.5), 0.0, 32767.0)
    coeff = jnp.where(c3 < 0.0, -level, level)
    low = lax.broadcasted_iota(jnp.int32, (32, 128), 1) < 64
    first = position % 2 == 0
    msg = jnp.where(
        low, coeff, jnp.where(first, pltpu.roll(place, 64, 1), place)
    ).astype(jnp.int32).astype(jnp.int16)
    for k in range(32):
        msg_out[k] = msg


def sibling_sum(c, left, right):
    chl = stacked(c)
    block = jnp.exp2(mm_tn(left, right))
    zero = jnp.zeros((128, 128), F32)
    rows = []
    for s in range(4):
        src = slice(128 * s, 128 * (s + 1))
        rows.append(jnp.concatenate(
            [zero if s == t else block[src, 128 * t:128 * (t + 1)] for t in range(4)], axis=1))
    hi, lo = halves(jnp.concatenate(rows, axis=0))
    return fold(mm(chl, hi)) + mm(chl[:32], lo)


def near_kernel(
    rhs, pts, basis, t_lower, t_upper, c0, s0, c1, s1, got, place3,
    near_out, t0_out, t1_out, t2_out, basis_out, above_out,
    rhs_v, pts_v, basis_v, above_v, c0_v, s0_v, near_v, sems, chunk_sems, out_sems,
):
    ahead = copies(
        [
            (t_lower, above_v.at[pl.ds(0, 4)]), (t_upper, above_v.at[pl.ds(4, 1)]),
        ], sems)

    def arrivals(step):
        cols = pl.ds(pl.multiple_of(step * 2048, 2048), 2048)
        return copies(
            [
                (pts.at[:, cols], pts_v.at[step]), (rhs.at[:, cols], rhs_v.at[step]),
                (c0.at[step], c0_v.at[step]), (s0.at[step], s0_v.at[step]),
                (basis.at[pl.ds(step * 4, 4)], basis_v.at[step]),
            ], chunk_sems, 5 * step)

    def departure(step):
        return pltpu.make_async_copy(near_v.at[step], near_out.at[step], out_sems.at[step])

    for step in range(4):
        for copy in arrivals(step):
            copy.start()
    for copy in ahead:
        copy.start()

    def chunk(step, carry):
        for copy in arrivals(step):
            copy.wait()
        for q in range(4):
            leaf = slice(512 * q, 512 * (q + 1))
            x = rhs_v[step, :, leaf]
            left, right = operands(*halves(pts_v[step, :, leaf] * SCALE))
            wide = jnp.exp2(mm_tn(left[:, :256], right)).astype(BF)
            last = jnp.exp2(mm_tn(left[:, 256:], right[:, 256:])).astype(BF)
            both = mm(x[:, :256], wide) + RIDGE * x.astype(F32)
            first = both[:, :256] + mm_nt(x[:, 256:], wide[:, 256:])
            second = both[:, 256:] + mm(x[:, 256:], last)
            near_v[step, :, leaf] = jnp.concatenate([first, second], axis=1).astype(BF)
        departure(step).start()
        for q in range(4):
            basis_out[4 * step + q] = basis_v[step, q].T
        t0_out[step] = sibling_sum(c0_v[step], *operands(s0_v[step, :32, :], s0_v[step, 32:, :]))
        return carry

    lax.fori_loop(0, 4, chunk, 0)
    t1_out[...] = sibling_sum(c1[...], *operands(s1[:32, :], s1[32:, :]))
    mine = lax.axis_index("leaf") % 4
    target, _ = operands(got[mine, 64:96, :], got[mine, 96:128, :])

    def side(rows):
        return jnp.concatenate([got[k, rows, :] for k in range(4)], axis=1)

    _, source = operands(side(slice(64, 96)), side(slice(96, 128)))
    hi, lo = halves(jnp.exp2(mm_tn(target, source)))
    c2 = jnp.concatenate(
        [jnp.where(mine == k, 0.0, got[k, 0:32, :].astype(F32)) for k in range(4)], axis=1
    ).astype(BF)
    t2_out[...] = mm_nt(c2, hi) + mm_nt(c2, lo)
    for copy in ahead:
        copy.wait()
    for k in range(5):
        above_out[:, 128 * k:128 * (k + 1)] = above_v[k].T
    for step in range(4):
        departure(step).wait()


def top_kernel(got, place3, near, t_leaf, out, near_out, tl_out, sems):
    ahead = copies([(t_leaf, tl_out), (near, near_out)], sems)
    for copy in ahead:
        copy.start()
    node = lax.axis_index("leaf") // 4
    _, target = operands(place3[:32, :], place3[32:, :])
    low = lax.broadcasted_iota(jnp.int32, (32, 128), 1) < 64
    column = lax.broadcasted_iota(jnp.int32, (32, 512), 1)
    acc = jnp.zeros((32, 128), F32)
    for first in range(0, 32, 8):
        coeffs, places = [], []
        for k in range(first, first + 8, 2):
            even = got[k].astype(jnp.int32).astype(F32)
            odd = got[k + 1].astype(jnp.int32).astype(F32)
            coeffs.append(jnp.where(low, even, pltpu.roll(odd, 64, 1)))
            places.append(jnp.where(low, pltpu.roll(even, 64, 1), odd))
        level = jnp.concatenate(coeffs, axis=1)
        size = jnp.exp2(jnp.abs(level) * (1.0 / LOG_STEPS) - LOG_ZERO)
        c3 = jnp.where(level < 0.0, -size, size)
        c3 = jnp.where((level == 0.0) | (column // 64 == node - first), 0.0, c3)
        place = jnp.concatenate(places, axis=1) * (1.0 / PLACE_STEPS)
        source, _ = operands(*halves(place))
        hi, lo = halves(jnp.exp2(mm_tn(source, target)))
        chl = stacked(c3)
        acc = acc + fold(mm(chl, hi)) + mm(chl[:32], lo)
    out[...] = acc
    for copy in ahead:
        copy.wait()


def down_kernel(
    part, other, t0, t1, t2, near, basis, t_leaf, above,
    out, out_v, out_sems,
):
    def departure(step):
        cols = pl.ds(pl.multiple_of(step * 2048, 2048), 2048)
        return pltpu.make_async_copy(out_v.at[step], out.at[:, cols], out_sems.at[step])

    t3 = part[...] + other[...]
    g2 = t2[...] + fold(mm(stacked(t3), above[:, 512:]))
    g1 = t1[...] + fold(mm(stacked(g2), above[:, :512]))
    g0 = []
    for step in range(4):
        here = stacked(g1[:, 128 * step:128 * (step + 1)])
        g0.append((t0[step] + fold(mm_nt(here, t_leaf[4 * step:4 * step + 4].reshape(512, 128)))).astype(BF))
    for step in range(4):
        for q in range(4):
            cols = slice(512 * q, 512 * (q + 1))
            far = mm(g0[step][:, 128 * q:128 * (q + 1)], basis[4 * step + q])
            out_v[step, :, cols] = (near[step, :, cols].astype(F32) + far).astype(BF)
        departure(step).start()
    for step in range(4):
        departure(step).wait()


def call(kernel, name, ins, outs, scratch=(), cost=None, **kwargs):
    spec = lambda space: pl.BlockSpec(memory_space=space)
    return pl.pallas_call(
        kernel,
        in_specs=[spec(space) for _, space in ins],
        out_specs=[spec(space) for _, _, space in outs],
        out_shape=[
            (space if space is not pl.ANY else jax.ShapeDtypeStruct)(shape, dtype)
            for shape, dtype, space in outs
        ],
        scratch_shapes=list(scratch),
        compiler_params=pltpu.CompilerParams(vmem_limit_bytes=VMEM_LIMIT),
        cost_estimate=cost,
        name=name,
    )(*[pltpu.with_memory_space_constraint(x, space) for x, space in ins])


def per_device(
    rhs_block, points, basis, skeleton_leaf, skeleton_lower, skeleton_upper,
    skeleton_top, transfer_leaf, transfer_lower, transfer_upper,
):
    vmem, hbm, dma = pltpu.VMEM, pltpu.HBM, pltpu.SemaphoreType.DMA
    i32 = jnp.int32

    def inside(*arrays):
        return [(x, vmem) for x in arrays]

    def outside(*arrays):
        return [(x, hbm) for x in arrays]

    transfers = (transfer_leaf, transfer_lower, transfer_upper)
    top_index, c0, s0, c1, s1, msg1 = call(
        up_kernel, "upward",
        outside(
            rhs_block, points, basis, skeleton_leaf, skeleton_lower, skeleton_upper,
            skeleton_top, *transfers),
        [
            ((32, 128), i32, vmem), ((4, 32, 512), F32, hbm), ((4, 64, 512), BF, hbm),
            ((32, 512), F32, vmem), ((64, 512), BF, vmem), ((4, 128, 128), BF, vmem),
        ],
        [
            vmem((4, 32, 2048), BF), vmem((4, 32, 2048), F32), vmem((4, 4, 512, 128), BF),
            vmem((4, 4, 128, 128), BF), vmem((4, 128, 128), BF), vmem((1, 128, 128), BF),
            vmem((16, 128), i32), vmem((4, 128), i32), vmem((1, 128), i32),
            vmem((4, 32, 512), F32), vmem((4, 64, 512), BF), dma((6,)), dma((16,)), dma((8,)),
        ],
        pl.CostEstimate(flops=10**9, bytes_accessed=5 * 10**6, transcendentals=0),
    )

    nodes = lax.axis_size("leaf") // 4
    siblings = [[4 * k + i for i in range(4)] for k in range(nodes)]
    turn = (0, 0, 1, 1)
    across = [
        [4 * k + 2 * (turn[k % 4] ^ chip) + core for k in range(nodes)]
        for chip in range(2) for core in range(2)
    ]
    got1 = lax.all_to_all(msg1, "leaf", 0, 0, axis_index_groups=siblings, tiled=True)

    msg2, place3 = call(
        mid_kernel, "middle", inside(got1, top_index),
        [((32, 32, 128), jnp.int16, vmem), ((64, 128), BF, vmem)],
    )

    got2 = lax.all_to_all(msg2, "leaf", 0, 0, axis_index_groups=across, tiled=True)

    near, t0, t1, t2, gens, above = call(
        near_kernel, "near",
        outside(rhs_block, points, basis, transfer_lower, transfer_upper, c0, s0)
        + inside(c1, s1, got1, place3),
        [
            ((4, 32, 2048), BF, hbm), ((4, 32, 512), F32, vmem),
            ((32, 512), F32, vmem), ((32, 128), F32, vmem),
            ((16, 128, 512), BF, vmem), ((128, 640), BF, vmem),
        ],
        [
            vmem((4, 32, 2048), BF), vmem((4, 32, 2048), F32), vmem((4, 4, 512, 128), BF),
            vmem((5, 128, 128), BF),
            vmem((4, 32, 512), F32), vmem((4, 64, 512), BF), vmem((4, 32, 2048), BF),
            dma((2,)), dma((20,)), dma((4,)),
        ],
        pl.CostEstimate(flops=6 * 10**9, bytes_accessed=3 * 10**6, transcendentals=5 * 10**6),
    )

    part, near, t_leaf = call(
        top_kernel, "top", inside(got2, place3) + outside(near, transfer_leaf),
        [((32, 128), F32, vmem), ((4, 32, 2048), BF, vmem), ((16, 128, 128), BF, vmem)],
        [dma((2,))],
    )

    partner = [(i, i ^ 1) for i in range(4 * nodes)]
    other = lax.ppermute(part, "leaf", partner)

    product, = call(
        down_kernel, "downward",
        inside(part, other, t0, t1, t2, near, gens, t_leaf, above),
        [((32, 8192), BF, hbm)],
        [
            vmem((4, 32, 2048), BF), dma((4,)),
        ],
        pl.CostEstimate(flops=2 * 10**9, bytes_accessed=5 * 10**6, transcendentals=10**6),
    )
    return product


def solution(mesh):
    return jax.shard_map(
        per_device,
        mesh=mesh,
        in_specs=(
            P("rhs", "leaf"),
            P(None, "leaf"),
            P("leaf", None, None),
            P("leaf", None),
            P("leaf", None),
            P("leaf", None),
            P(),
            P("leaf", None, None),
            P("leaf", None, None),
            P("leaf", None, None),
        ),
        out_specs=P("rhs", "leaf"),
        check_vma=False,
    )
```
